128 devices in a mesh: az: 8 (over z, x_lo), rg: 16 (over y, x_hi, core).
Axes of the slice: x: 4 (x_hi: 2, x_lo: 2; x = x_hi * 2 + x_lo), y: 4, z: 4, core: 2. Of those that a mesh axis runs over, the one named last changes fastest.
Arguments:
- slab_echoes: bfloat16 [2, 2048, 16384], P(None, ('az', 'rg')), may hold values from -6 to 6
- fresh_pulses: bfloat16 [2, 6144, 16384], P(None, ('az', 'rg')), may hold values from -6 to 6
- range_filter: float32 [2, 16384], replicated, may hold values from -5 to 5
- azimuth_filter: bfloat16 [2, 8192, 16384], P(None, None, ('az', 'rg')), may hold values from -5 to 5
- migration_taps: float32 [9, 8192], replicated, may hold values from -2.4 to 2.4
- band_offsets: int32 [16384], P(('az', 'rg')), may hold values from 0 to 56
- band_widths: int32 [16384], P(('az', 'rg')), may hold values from 1 to 9
Outputs:
- focused_image: bfloat16 [2, 6144, 16384], P(None, ('az', 'rg'))
The draws below stay inside these ranges and needn't reach their ends.
All inputs are finite; a program needn't handle non-finite values.
Results may differ from the reference program's by a relative error of at most 0.019.
Values may be sent and summed in bfloat16 or wider, within the bound.
No kernel may reach another device: no remote copies, remote signals or barrier semaphores. Data moves between devices by JAX's collectives and lax.ppermute only.
A program may use at most 192 MiB of HBM per device.

```python
import math
import jax
import jax.numpy as jnp
from jax import lax

RANGE_OUTER = 128
RANGE_INNER = 128
PULSE_OUTER = 128
PULSE_INNER = 64
SLAB_PULSES = 2048
SHIFT_MAX = 56
BAND_MAX = 9
RANGE_BINS = 16384
PULSES = 8192
FRESH_COUNT = 6144
RIM_WIDTH = 64


def place_ends(values, key, least, largest):
    longest = values.shape.index(max(values.shape))
    spots = []
    for shift in (0, 1):
        where = [jax.random.randint(jax.random.fold_in(key, axis), (), 0, length) for axis, length in enumerate(values.shape)]
        where[longest] = (where[longest] + shift) % values.shape[longest]
        spots.append(tuple(where))
    return values.at[spots[0]].set(least).at[spots[1]].set(largest)


def block_scale(stream_key, dims, pieces, least, high):
    level = 1.0
    for axis_at, shards_of in pieces:
        heights = jax.random.uniform(jax.random.fold_in(jax.random.fold_in(stream_key, 6), axis_at), (shards_of,), jnp.float32, least / len(pieces), high / len(pieces))
        level = level * jnp.repeat(jnp.exp(heights), dims[axis_at] // shards_of).reshape((-1,) + (1,) * (len(dims) - 1 - axis_at))
    return level


def bell_draw(rng, shape, deviation, bound, cuts=(), kind=jnp.bfloat16):
    values = deviation * jax.random.normal(rng, shape, jnp.float32)
    if cuts:
        values = values * block_scale(rng, shape, cuts, -0.22, 0.18)
    return jnp.clip(values, -bound, bound).astype(kind)


def setup_inputs(seed: int = 0) -> dict:
    splits = jax.random.split(jax.random.key(seed), 8)
    slab_echoes = bell_draw(splits[0], (2, SLAB_PULSES, RANGE_BINS), 1.0, 6.0, ((1, 128),))
    fresh_pulses = bell_draw(splits[1], (2, FRESH_COUNT, RANGE_BINS), 1.0, 6.0, ((1, 128),))
    range_filter = bell_draw(splits[2], (2, RANGE_BINS), 0.7071, 5.0, (), jnp.float32)
    azimuth_filter = bell_draw(splits[3], (2, PULSES, RANGE_BINS), 0.7071, 5.0, ((2, 128),))
    migration_taps = bell_draw(splits[4], (BAND_MAX, PULSES), 0.4, 2.4, (), jnp.float32)
    band_offsets = place_ends(jax.random.randint(splits[5], (RANGE_BINS,), 0, SHIFT_MAX + 1), jax.random.fold_in(splits[5], 1), 0, SHIFT_MAX).astype(jnp.int32)
    band_widths = place_ends(jax.random.randint(splits[6], (RANGE_BINS,), 1, BAND_MAX + 1), jax.random.fold_in(splits[6], 1), 1, BAND_MAX).astype(jnp.int32)
    return dict(slab_echoes=slab_echoes, fresh_pulses=fresh_pulses, range_filter=range_filter, azimuth_filter=azimuth_filter, migration_taps=migration_taps, band_offsets=band_offsets, band_widths=band_widths)


def dft_table(length, sign):
    index = jnp.arange(length, dtype=jnp.int32)
    angle = (index[:, None] * index[None, :] % length).astype(jnp.float32) * (2.0 * math.pi / length)
    scale = 1.0 / math.sqrt(length)
    real_part = jnp.cos(angle) * scale
    imag_part = sign * jnp.sin(angle) * scale
    upper = jnp.stack([real_part, imag_part], axis=1)
    lower = jnp.stack([-imag_part, real_part], axis=1)
    return jnp.stack([upper, lower], axis=0).astype(jnp.bfloat16)

def twiddle(rows_size, cols_size, total, sign):
    left = jnp.arange(rows_size, dtype=jnp.int32)[:, None]
    right = jnp.arange(cols_size, dtype=jnp.int32)[None, :]
    angle = (left * right % total).astype(jnp.float32) * (2.0 * math.pi / total)
    return (jnp.cos(angle), sign * jnp.sin(angle))

def complex_mul(values, real_part, imag_part):
    return jnp.stack([values[0] * real_part - values[1] * imag_part, values[0] * imag_part + values[1] * real_part])

def range_compress(pulse_rows, range_filter):
    pulse_count = pulse_rows.shape[1]
    folded = pulse_rows.reshape(2, pulse_count, RANGE_OUTER, RANGE_INNER).astype(jnp.float32)
    partial_value = jnp.einsum('cpab,cadk->dpkb', folded, dft_table(RANGE_OUTER, -1.0).astype(jnp.float32))
    twist_re, twist_im = twiddle(RANGE_OUTER, RANGE_INNER, RANGE_BINS, -1.0)
    turned = complex_mul(partial_value, twist_re, twist_im).astype(jnp.bfloat16)
    spectrum = jnp.einsum('cpkb,cbdm->dpmk', turned.astype(jnp.float32), dft_table(RANGE_INNER, -1.0).astype(jnp.float32))
    shaped = range_filter.reshape(2, RANGE_INNER, RANGE_OUTER)
    matched = complex_mul(spectrum, shaped[0], shaped[1]).astype(jnp.bfloat16)
    inverse_part = jnp.einsum('cpmk,cmdb->dpkb', matched.astype(jnp.float32), dft_table(RANGE_INNER, 1.0).astype(jnp.float32))
    untwist_re, untwist_im = twiddle(RANGE_OUTER, RANGE_INNER, RANGE_BINS, 1.0)
    unturned = complex_mul(inverse_part, untwist_re, untwist_im).astype(jnp.bfloat16)
    result = jnp.einsum('cpkb,ckda->dpab', unturned.astype(jnp.float32), dft_table(RANGE_OUTER, 1.0).astype(jnp.float32))
    return result.reshape(2, pulse_count, RANGE_BINS).astype(jnp.bfloat16)

def azimuth_forward(columns, filter_cols):
    local_bins = columns.shape[2]
    folded = columns.reshape(2, PULSE_OUTER, PULSE_INNER, local_bins).astype(jnp.float32)
    partial_value = jnp.einsum('cblr,cbdk->dklr', folded, dft_table(PULSE_OUTER, -1.0).astype(jnp.float32))
    twist_re, twist_im = twiddle(PULSE_OUTER, PULSE_INNER, PULSES, -1.0)
    turned = complex_mul(partial_value, twist_re[:, :, None], twist_im[:, :, None]).astype(jnp.bfloat16)
    spectrum = jnp.einsum('cklr,cldm->dmkr', turned.astype(jnp.float32), dft_table(PULSE_INNER, -1.0).astype(jnp.float32))
    spectrum = spectrum.reshape(2, PULSES, local_bins)
    return complex_mul(spectrum, filter_cols[0].astype(jnp.float32), filter_cols[1].astype(jnp.float32)).astype(jnp.bfloat16)

def azimuth_inverse(columns):
    local_bins = columns.shape[2]
    folded = columns.reshape(2, PULSE_INNER, PULSE_OUTER, local_bins).astype(jnp.float32)
    partial_value = jnp.einsum('cmkr,cmdl->dlkr', folded, dft_table(PULSE_INNER, 1.0).astype(jnp.float32))
    twist_re, twist_im = twiddle(PULSE_INNER, PULSE_OUTER, PULSES, 1.0)
    turned = complex_mul(partial_value, twist_re[:, :, None], twist_im[:, :, None]).astype(jnp.bfloat16)
    outer_table = dft_table(PULSE_OUTER, 1.0)[:, :, :, SLAB_PULSES // PULSE_INNER:].astype(jnp.float32)
    focused = jnp.einsum('clkr,ckdb->dblr', turned.astype(jnp.float32), outer_table)
    return focused.reshape(2, FRESH_COUNT, local_bins).astype(jnp.bfloat16)

def migrate(extended, band_offsets, band_widths, migration_taps):
    local_bins = band_offsets.shape[0]
    starts = jnp.arange(local_bins, dtype=jnp.int32) + band_offsets.astype(jnp.int32)
    total = jnp.zeros((2, PULSES, local_bins), jnp.float32)
    for tap_index in range(BAND_MAX):
        picked = jnp.take(extended, starts + tap_index, axis=2)
        active = (band_widths > tap_index).astype(jnp.float32)
        weight = migration_taps[tap_index][:, None] * active[None, :]
        total = total + picked.astype(jnp.float32) * weight[None]
    return total.astype(jnp.bfloat16)

def by_columns(function, arrays, column_block):
    groups = RANGE_BINS // column_block
    stacked = tuple((jnp.moveaxis(source_array.reshape(source_array.shape[:-1] + (groups, column_block)), -2, 0) for source_array in arrays))
    mapped = lax.map(lambda members: function(*members), stacked)
    moved = jnp.moveaxis(mapped, 0, -2)
    return moved.reshape(moved.shape[:-2] + (RANGE_BINS,))

def reference(slab_echoes, fresh_pulses, range_filter, azimuth_filter, migration_taps, band_offsets, band_widths):
    pulse_rows = jnp.concatenate([slab_echoes, fresh_pulses], axis=1)
    pulse_block = math.gcd(PULSES, 512)
    blocks = pulse_rows.reshape(2, PULSES // pulse_block, pulse_block, RANGE_BINS).transpose(1, 0, 2, 3)
    compressed = lax.map(lambda pulse_group: range_compress(pulse_group, range_filter), blocks)
    compressed = compressed.transpose(1, 0, 2, 3).reshape(2, PULSES, RANGE_BINS)
    column_block = math.gcd(RANGE_BINS, 512)
    spectra = by_columns(azimuth_forward, (compressed, azimuth_filter), column_block)
    extended = jnp.concatenate([spectra, jnp.zeros((2, PULSES, RIM_WIDTH), jnp.bfloat16)], axis=2)
    migrated = migrate(extended, band_offsets, band_widths, migration_taps)
    return by_columns(azimuth_inverse, (migrated,), column_block)
```

```python
import functools
import math

import jax
import jax.numpy as jnp
import ml_dtypes
import numpy as np
from jax import lax
from jax.experimental import pallas as pl
from jax.experimental.pallas import tpu as pltpu
from jax.sharding import PartitionSpec as P

RANGE_OUTER = 128
RANGE_INNER = 128
PULSE_OUTER = 128
PULSE_INNER = 64
SLAB_PULSES = 2048
BAND_MAX = 9
RANGE_BINS = 16384
PULSES = 8192
FRESH_COUNT = 6144
LANES = 128
HALF = 64
DEVICES = 128
SLAB_ROWS = SLAB_PULSES // DEVICES
FRESH_ROWS = FRESH_COUNT // DEVICES
ROWS = SLAB_ROWS + FRESH_ROWS
STEP = 16
FIRST_OUTER = SLAB_PULSES // PULSE_INNER
KEPT_OUTER = PULSE_OUTER - FIRST_OUTER
GROUP = 4
AXES = ("az", "rg")
MIB = 1024 * 1024


def bf16(values):
    return np.asarray(values, np.float32).astype(ml_dtypes.bfloat16)


def dft_table(length, sign):
    index = np.arange(length)
    angle = (np.outer(index, index) % length).astype(np.float32) * np.float32(
        2.0 * math.pi / length
    )
    scale = np.float32(1.0 / math.sqrt(length))
    real_part = bf16(np.cos(angle) * scale).astype(np.float32)
    imag_part = bf16(sign * np.sin(angle) * scale).astype(np.float32)
    return real_part, imag_part


def twiddle(rows_size, cols_size, total, sign):
    angle = (np.outer(np.arange(rows_size), np.arange(cols_size)) % total).astype(
        np.float32
    ) * np.float32(2.0 * math.pi / total)
    return np.cos(angle), np.float32(sign) * np.sin(angle)


def left_table(length, sign):
    re, im = dft_table(length, sign)
    return bf16(np.block([[re, -im], [im, re]]))


def right_table(length, sign):
    re, im = dft_table(length, sign)
    return bf16(np.block([[re, im], [-im, re]]))


def turned_tables(outer, inner, sign):
    re, im = dft_table(outer, sign)
    tw_re, tw_im = twiddle(outer, inner, PULSES, sign)
    turn_re, turn_im = tw_re.T[:, :, None], tw_im.T[:, :, None]
    return bf16(
        np.concatenate(
            [re * turn_re - im * turn_im, re * turn_im + im * turn_re], axis=2
        )
    )


def roll_half(values):
    return pltpu.roll(values, HALF, 1)


def lane_ids(rows):
    return lax.broadcasted_iota(jnp.int32, (rows, LANES), 1)


def times_i(values):
    turned = roll_half(values)
    return jnp.where(lane_ids(values.shape[0]) < HALF, -turned, turned)


def dot(left, right):
    return jnp.dot(left, right, preferred_element_type=jnp.float32)


def range_kernel(slab, fresh, filt, t1, t2, t3, t4, w_in, w_out, out0, out1, xs, os, hs):
    step = pl.program_id(0)

    def load(source):
        def one(n1, _):
            at = pl.ds(pl.multiple_of(n1 * LANES, LANES), LANES)
            to = pl.ds(pl.multiple_of(n1 * STEP, STEP), STEP)
            for c in range(2):
                xs[c, to, :] = source[c, :, at].astype(jnp.float32)
            return 0

        lax.fori_loop(0, RANGE_OUTER, one, 0, unroll=8)

    @pl.when(step == 0)
    def _():
        hs[0] = filt[0].T
        hs[1] = filt[1].T
        load(slab)

    @pl.when(step > 0)
    def _():
        load(fresh)

    def rows(p):
        return pl.ds(p, RANGE_OUTER, stride=STEP)

    def pair(i, _):
        ps = (2 * i, 2 * i + 1)
        x = jnp.concatenate(
            [
                jnp.concatenate([xs[c, rows(p), :].astype(jnp.bfloat16) for p in ps], axis=1)
                for c in range(2)
            ],
            axis=0,
        )
        y = dot(t1[...], x)
        parts = []
        for k in range(2):
            re, im = y[:LANES, k * LANES : (k + 1) * LANES], y[LANES:, k * LANES : (k + 1) * LANES]
            parts.append(
                jnp.concatenate(
                    [
                        (re * w_in[0] - im * w_in[1]).astype(jnp.bfloat16),
                        (re * w_in[1] + im * w_in[0]).astype(jnp.bfloat16),
                    ],
                    axis=1,
                )
            )
        y = dot(jnp.concatenate(parts, axis=0), t2[...])
        parts = []
        for k in range(2):
            re, im = y[k * LANES : (k + 1) * LANES, :LANES], y[k * LANES : (k + 1) * LANES, LANES:]
            parts.append(
                jnp.concatenate(
                    [
                        (re * hs[0] - im * hs[1]).astype(jnp.bfloat16),
                        (re * hs[1] + im * hs[0]).astype(jnp.bfloat16),
                    ],
                    axis=1,
                )
            )
        y = dot(jnp.concatenate(parts, axis=0), t3[...])
        parts = []
        for k in range(2):
            re, im = y[k * LANES : (k + 1) * LANES, :LANES], y[k * LANES : (k + 1) * LANES, LANES:]
            parts.append(
                jnp.concatenate(
                    [
                        (re * w_out[0] - im * w_out[1]).astype(jnp.bfloat16),
                        (re * w_out[1] + im * w_out[0]).astype(jnp.bfloat16),
                    ],
                    axis=0,
                )
            )
        y = dot(t4[...], jnp.concatenate(parts, axis=1))
        low = lane_ids(LANES) < HALF
        for k, p in enumerate(ps):
            re, im = y[:LANES, k * LANES : (k + 1) * LANES], y[LANES:, k * LANES : (k + 1) * LANES]
            os[0, rows(p), :] = jnp.where(low, re, roll_half(im))
            os[1, rows(p), :] = jnp.where(low, roll_half(re), im)
        return 0

    lax.fori_loop(0, STEP // 2, pair, 0)

    def store(n1, _):
        at = pl.ds(pl.multiple_of(n1 * STEP, STEP), STEP)
        out0[n1] = os[0, at, :].astype(jnp.bfloat16)
        out1[n1] = os[1, at, :].astype(jnp.bfloat16)
        return 0

    lax.fori_loop(0, RANGE_OUTER, store, 0, unroll=8)


def whole(shape):
    return pl.BlockSpec(shape, lambda *_: (0,) * len(shape))


def range_compress(slab, fresh, range_filter):
    filt = range_filter.reshape(2, RANGE_INNER, RANGE_OUTER)
    tables = (
        left_table(RANGE_OUTER, -1.0),
        right_table(RANGE_INNER, -1.0),
        right_table(RANGE_INNER, 1.0),
        left_table(RANGE_OUTER, 1.0),
    )
    w_in = np.stack(twiddle(RANGE_OUTER, RANGE_INNER, RANGE_BINS, -1.0))
    w_out = np.stack(twiddle(RANGE_OUTER, RANGE_INNER, RANGE_BINS, 1.0))
    square = whole((2 * LANES, 2 * LANES))
    part = whole((2, LANES, LANES))
    out = jax.ShapeDtypeStruct((DEVICES, ROWS, LANES), jnp.bfloat16)
    return pl.pallas_call(
        range_kernel,
        grid=(ROWS // STEP,),
        in_specs=[
            whole((2, STEP, RANGE_BINS)),
            pl.BlockSpec((2, STEP, RANGE_BINS), lambda i: (0, jnp.maximum(i - 1, 0), 0)),
            part,
            square,
            square,
            square,
            square,
            part,
            part,
        ],
        out_specs=[pl.BlockSpec((DEVICES, STEP, LANES), lambda i: (0, i, 0))] * 2,
        out_shape=[out, out],
        scratch_shapes=[
            pltpu.VMEM((2, RANGE_OUTER * STEP, LANES), jnp.float32),
            pltpu.VMEM((2, RANGE_OUTER * STEP, LANES), jnp.float32),
            pltpu.VMEM((2, LANES, LANES), jnp.float32),
        ],
        compiler_params=pltpu.CompilerParams(
            dimension_semantics=("arbitrary",), vmem_limit_bytes=32 * MIB
        ),
        cost_estimate=pl.CostEstimate(
            flops=4 * 2 * ROWS * RANGE_BINS * 512, bytes_accessed=8 * MIB, transcendentals=0
        ),
        name="range_compress",
    )(slab, fresh, filt, *tables, w_in, w_out)


def filter_kernel(filt, out, fs):
    for c in range(2):
        for kl in range(PULSE_INNER):
            fs[c, kl * STEP : (kl + 1) * STEP, :] = filt[c, kl].astype(jnp.float32)
    low = lane_ids(PULSE_INNER) < HALF
    for kb in range(STEP):
        for c in range(2):
            value = fs[c, pl.ds(kb, PULSE_INNER, stride=STEP), :]
            turned = roll_half(value)
            at = slice(kb * PULSE_INNER, (kb + 1) * PULSE_INNER)
            out[0, c, at, :] = jnp.where(low, value, turned).astype(jnp.bfloat16)
            out[1, c, at, :] = jnp.where(low, turned, value).astype(jnp.bfloat16)


def filter_by_outer(azimuth_filter):
    folded = azimuth_filter.reshape(2, PULSE_INNER, PULSE_OUTER, LANES)
    return pl.pallas_call(
        filter_kernel,
        grid=(PULSE_OUTER // STEP,),
        in_specs=[pl.BlockSpec((2, PULSE_INNER, STEP, LANES), lambda i: (0, 0, i, 0))],
        out_specs=pl.BlockSpec((2, 2, STEP * PULSE_INNER, LANES), lambda i: (0, 0, i, 0)),
        out_shape=jax.ShapeDtypeStruct((2, 2, PULSES, LANES), jnp.bfloat16),
        scratch_shapes=[pltpu.VMEM((2, PULSE_INNER * STEP, LANES), jnp.float32)],
        compiler_params=pltpu.CompilerParams(
            dimension_semantics=("arbitrary",), vmem_limit_bytes=24 * MIB
        ),
        cost_estimate=pl.CostEstimate(
            flops=8 * PULSES * LANES, bytes_accessed=12 * MIB, transcendentals=0
        ),
        name="filter_by_outer",
    )(folded)


def forward_kernel(got, g1, t2, filt, out, ps, ts):
    def unpack(s, _):
        block = got[s].astype(jnp.float32)
        ps[pl.ds(pl.multiple_of(s * SLAB_ROWS, SLAB_ROWS), SLAB_ROWS), :] = block[:SLAB_ROWS]
        at = pl.multiple_of(SLAB_PULSES + s * FRESH_ROWS, STEP)
        ps[pl.ds(at, FRESH_ROWS), :] = block[SLAB_ROWS:]
        return 0

    lax.fori_loop(0, DEVICES, unpack, 0, unroll=4)

    def outer(l, _):
        x = ps[pl.ds(l, PULSE_OUTER, stride=PULSE_INNER), :]
        both = jnp.concatenate([x.astype(jnp.bfloat16), times_i(x).astype(jnp.bfloat16)], axis=0)
        ts[pl.ds(l, PULSE_OUTER, stride=PULSE_INNER), :] = dot(g1[l], both)
        return 0

    lax.fori_loop(0, PULSE_INNER, outer, 0, unroll=4)

    def inner(i, _):
        sides = []
        for k in range(2):
            at = pl.ds(pl.multiple_of((2 * i + k) * PULSE_INNER, PULSE_INNER), PULSE_INNER)
            t = ts[at, :]
            sides.append(
                jnp.concatenate([t.astype(jnp.bfloat16), times_i(t).astype(jnp.bfloat16)], axis=0)
            )
        y = dot(t2[...], jnp.concatenate(sides, axis=1))
        for k in range(2):
            at = pl.ds(pl.multiple_of((2 * i + k) * PULSE_INNER, PULSE_INNER), PULSE_INNER)
            cols = slice(k * LANES, (k + 1) * LANES)
            out[at, :] = (
                y[:PULSE_INNER, cols] * filt[0, 0, at, :].astype(jnp.float32)
                + y[PULSE_INNER:, cols] * filt[0, 1, at, :].astype(jnp.float32)
            ).astype(jnp.bfloat16)
        return 0

    lax.fori_loop(0, PULSE_OUTER // 2, inner, 0, unroll=4)


def azimuth_forward(got, filt, half):
    g1 = turned_tables(PULSE_OUTER, PULSE_INNER, -1.0)
    re, im = dft_table(PULSE_INNER, -1.0)
    t2 = bf16(np.block([[re, im], [-im, re]]))
    return pl.pallas_call(
        forward_kernel,
        grid=(1,),
        in_specs=[
            whole((DEVICES, ROWS, LANES)),
            whole(g1.shape),
            whole(t2.shape),
            pl.BlockSpec((1, 2, PULSES, LANES), lambda i: (half, 0, 0, 0)),
        ],
        out_specs=whole((PULSES, LANES)),
        out_shape=jax.ShapeDtypeStruct((PULSES, LANES), jnp.bfloat16),
        scratch_shapes=[
            pltpu.VMEM((PULSES, LANES), jnp.float32),
            pltpu.VMEM((PULSES, LANES), jnp.float32),
        ],
        compiler_params=pltpu.CompilerParams(
            dimension_semantics=("arbitrary",), vmem_limit_bytes=40 * MIB
        ),
        cost_estimate=pl.CostEstimate(
            flops=2 * PULSES * LANES * 512, bytes_accessed=12 * MIB, transcendentals=0
        ),
        name="azimuth_forward",
    )(got, g1, t2, filt)


def inverse_kernel(left, right, taps, bands, g1, t2, out, sel, vs, os):
    index = lax.broadcasted_iota(jnp.int32, (2 * LANES, LANES), 0)
    lane = lax.broadcasted_iota(jnp.int32, (2 * LANES, LANES), 1)
    column = jnp.where(index >= LANES, HALF, 0) + (index & (HALF - 1))
    same = ((index >> 6) & 1) == (lane >> 6)
    want = (lane & (HALF - 1)) + bands[0:1, :]
    for j in range(BAND_MAX):
        hit = same & (column == want + j) & (bands[1:2, :] > j)
        sel[:, j * LANES : (j + 1) * LANES] = jnp.where(hit, 1.0, 0.0).astype(jnp.bfloat16)

    size = GROUP * PULSE_INNER

    def group(g, _):
        at = pl.ds(pl.multiple_of(g * size, size), size)
        source = jnp.concatenate([left[at, :], right[at, :]], axis=1)
        total = None
        for j in range(0, BAND_MAX, 2):
            wide = min(2, BAND_MAX - j)
            picked = dot(source, sel[:, j * LANES : (j + wide) * LANES])
            for k in range(wide):
                term = picked[:, k * LANES : (k + 1) * LANES] * taps[at, j + k : j + k + 1]
                total = term if total is None else total + term
        here = total.astype(jnp.bfloat16)
        turned = times_i(total).astype(jnp.bfloat16)
        for k in range(GROUP):
            kb = g * GROUP + k
            rows = slice(k * PULSE_INNER, (k + 1) * PULSE_INNER)
            both = jnp.concatenate([here[rows], turned[rows]], axis=0)
            vs[pl.ds(kb, PULSE_INNER, stride=PULSE_OUTER), :] = dot(g1[kb], both)
        return 0

    lax.fori_loop(0, PULSE_OUTER // GROUP, group, 0)

    def last(i, _):
        sides = []
        for k in range(2):
            at = pl.ds(pl.multiple_of((2 * i + k) * PULSE_OUTER, PULSE_OUTER), PULSE_OUTER)
            v = vs[at, :]
            sides.append(
                jnp.concatenate([v.astype(jnp.bfloat16), times_i(v).astype(jnp.bfloat16)], axis=0)
            )
        y = dot(t2[...], jnp.concatenate(sides, axis=1))
        for k in range(2):
            os[pl.ds(2 * i + k, KEPT_OUTER, stride=PULSE_INNER), :] = y[
                :, k * LANES : (k + 1) * LANES
            ]
        return 0

    lax.fori_loop(0, PULSE_INNER // 2, last, 0, unroll=2)

    def pack(d, _):
        at = pl.ds(pl.multiple_of(d * FRESH_ROWS, STEP), FRESH_ROWS)
        out[d] = os[at, :].astype(jnp.bfloat16)
        return 0

    lax.fori_loop(0, DEVICES, pack, 0, unroll=4)


def azimuth_inverse(left, right, taps, bands):
    g1 = turned_tables(PULSE_INNER, PULSE_OUTER, 1.0)
    re, im = dft_table(PULSE_OUTER, 1.0)
    t2 = bf16(np.concatenate([re[FIRST_OUTER:], im[FIRST_OUTER:]], axis=1))
    return pl.pallas_call(
        inverse_kernel,
        grid=(1,),
        in_specs=[
            whole((PULSES, LANES)),
            whole((PULSES, LANES)),
            whole((PULSES, BAND_MAX)),
            whole((2, LANES)),
            whole(g1.shape),
            whole(t2.shape),
        ],
        out_specs=whole((DEVICES, FRESH_ROWS, LANES)),
        out_shape=jax.ShapeDtypeStruct((DEVICES, FRESH_ROWS, LANES), jnp.bfloat16),
        scratch_shapes=[
            pltpu.VMEM((2 * LANES, BAND_MAX * LANES), jnp.bfloat16),
            pltpu.VMEM((PULSES, LANES), jnp.float32),
            pltpu.VMEM((FRESH_COUNT, LANES), jnp.float32),
        ],
        compiler_params=pltpu.CompilerParams(
            dimension_semantics=("arbitrary",), vmem_limit_bytes=44 * MIB
        ),
        cost_estimate=pl.CostEstimate(
            flops=2 * PULSES * LANES * (256 * BAND_MAX + 512),
            bytes_accessed=12 * MIB,
            transcendentals=0,
        ),
        name="migrate_inverse",
    )(left, right, taps, bands, g1, t2)


def assemble_kernel(first, second, out):
    low = lane_ids(FRESH_ROWS) < HALF

    def one(n1, _):
        a, b = first[n1].astype(jnp.float32), second[n1].astype(jnp.float32)
        at = pl.ds(pl.multiple_of(n1 * LANES, LANES), LANES)
        out[0, :, at] = jnp.where(low, a, roll_half(b)).astype(jnp.bfloat16)
        out[1, :, at] = jnp.where(low, roll_half(a), b).astype(jnp.bfloat16)
        return 0

    lax.fori_loop(0, first.shape[0], one, 0, unroll=4)


def assemble(first, second):
    block = 32
    return pl.pallas_call(
        assemble_kernel,
        grid=(RANGE_OUTER // block,),
        in_specs=[pl.BlockSpec((block, FRESH_ROWS, LANES), lambda i: (i, 0, 0))] * 2,
        out_specs=pl.BlockSpec((2, FRESH_ROWS, block * LANES), lambda i: (0, 0, i)),
        out_shape=jax.ShapeDtypeStruct((2, FRESH_ROWS, RANGE_BINS), jnp.bfloat16),
        compiler_params=pltpu.CompilerParams(
            dimension_semantics=("arbitrary",), vmem_limit_bytes=24 * MIB
        ),
        cost_estimate=pl.CostEstimate(
            flops=4 * FRESH_ROWS * RANGE_BINS, bytes_accessed=6 * MIB, transcendentals=0
        ),
        name="assemble",
    )(first, second)


def exchanged(blocks):
    return lax.all_to_all(blocks, AXES, split_axis=0, concat_axis=0, tiled=True)


def from_next(block):
    size = lax.axis_size(AXES)
    return lax.ppermute(block, AXES, [(i + 1, i) for i in range(size - 1)])


def on_device(
    slab_echoes,
    fresh_pulses,
    range_filter,
    azimuth_filter,
    migration_taps,
    band_offsets,
    band_widths,
):
    packed0, packed1 = range_compress(slab_echoes, fresh_pulses, range_filter)
    filt = filter_by_outer(azimuth_filter)
    taps = migration_taps.reshape(BAND_MAX, PULSE_INNER, PULSE_OUTER)
    taps = taps.transpose(2, 1, 0).reshape(PULSES, BAND_MAX)
    bands = jnp.stack([band_offsets, band_widths]).reshape(2, 2, 1, HALF)
    bands = jnp.broadcast_to(bands, (2, 2, 2, HALF)).reshape(2, 2, LANES)
    spectra0 = azimuth_forward(exchanged(packed0), filt, 0)
    rim = from_next(spectra0)
    spectra1 = azimuth_forward(exchanged(packed1), filt, 1)
    done0 = exchanged(azimuth_inverse(spectra0, spectra1, taps, bands[:, 0]))
    done1 = exchanged(azimuth_inverse(spectra1, rim, taps, bands[:, 1]))
    return assemble(done0, done1)


def solution(mesh):
    placed = (
        P(None, AXES, None),
        P(None, AXES, None),
        P(),
        P(None, None, AXES),
        P(),
        P(AXES),
        P(AXES),
    )
    return jax.shard_map(
        on_device,
        mesh=mesh,
        in_specs=placed,
        out_specs=P(None, AXES, None),
        check_vma=False,
    )
```

```python
import functools
import math

import jax
import jax.numpy as jnp
import ml_dtypes
import numpy as np
from jax import lax
from jax.experimental import pallas as pl
from jax.experimental.pallas import tpu as pltpu
from jax.sharding import PartitionSpec as P

RANGE_OUTER = 128
RANGE_INNER = 128
PULSE_OUTER = 128
PULSE_INNER = 64
SLAB_PULSES = 2048
BAND_MAX = 9
RANGE_BINS = 16384
PULSES = 8192
FRESH_COUNT = 6144
LANES = 128
HALF = 64
DEVICES = 128
SLAB_ROWS = SLAB_PULSES // DEVICES
FRESH_ROWS = FRESH_COUNT // DEVICES
ROWS = SLAB_ROWS + FRESH_ROWS
STEP = 16
FIRST_OUTER = SLAB_PULSES // PULSE_INNER
KEPT_OUTER = PULSE_OUTER - FIRST_OUTER
GROUP = 4
UNROLL = 8
PITCH = STEP + 8
INNER_PITCH = PULSE_INNER + 8
OUTER_PITCH = PULSE_OUTER + 8
BLOCKS = ROWS // STEP
RANGE_LIMIT = 60
FWD_LIMIT = 60
INV_LIMIT = 60
PARTS = 4
ASSEMBLE = 32
AXES = ("az", "rg")
MIB = 1024 * 1024


def bf16(values):
    return np.asarray(values, np.float32).astype(ml_dtypes.bfloat16)


def dft_table(length, sign):
    index = np.arange(length)
    angle = (np.outer(index, index) % length).astype(np.float32) * np.float32(
        2.0 * math.pi / length
    )
    scale = np.float32(1.0 / math.sqrt(length))
    real_part = bf16(np.cos(angle) * scale).astype(np.float32)
    imag_part = bf16(sign * np.sin(angle) * scale).astype(np.float32)
    return real_part, imag_part


def twiddle(rows_size, cols_size, total, sign):
    angle = (np.outer(np.arange(rows_size), np.arange(cols_size)) % total).astype(
        np.float32
    ) * np.float32(2.0 * math.pi / total)
    return np.cos(angle), np.float32(sign) * np.sin(angle)


def left_table(length, sign):
    re, im = dft_table(length, sign)
    return bf16(np.block([[re, -im], [im, re]]))


def right_table(length, sign):
    re, im = dft_table(length, sign)
    return bf16(np.block([[re, im], [-im, re]]))


def turned_tables(outer, inner, sign):
    re, im = dft_table(outer, sign)
    tw_re, tw_im = twiddle(outer, inner, PULSES, sign)
    turn_re, turn_im = tw_re.T[:, :, None], tw_im.T[:, :, None]
    return bf16(
        np.concatenate(
            [re * turn_re - im * turn_im, re * turn_im + im * turn_re], axis=2
        )
    )


def turn_table():
    one = np.eye(HALF, dtype=np.float32)
    return bf16(np.block([[0 * one, one], [-one, 0 * one]]))


def roll_half(values):
    return pltpu.roll(values, HALF, 1)


def lane_ids(rows):
    return lax.broadcasted_iota(jnp.int32, (rows, LANES), 1)


def times_i(values):
    turned = roll_half(values)
    return jnp.where(lane_ids(values.shape[0]) < HALF, -turned, turned)


def dot(left, right):
    return jnp.dot(left, right, preferred_element_type=jnp.float32)


def in_vmem():
    return pl.BlockSpec(memory_space=pltpu.VMEM)


def in_hbm():
    return pl.BlockSpec(memory_space=pl.ANY)


def range_kernel(slab, fresh, filt, t1, t2, t3, t4, w_in, w_out, out, xs, os, hs, first, second, third):
    step = pl.program_id(0)

    def load(source):
        def one(n1, _):
            at = pl.ds(pl.multiple_of(n1 * LANES, LANES), LANES)
            to = pl.ds(pl.multiple_of(n1 * PITCH, 8), STEP)
            for c in range(2):
                xs[c, to, :] = source[c, :, at].astype(jnp.float32)
            return 0

        lax.fori_loop(0, RANGE_OUTER, one, 0, unroll=8)

    @pl.when(step == 0)
    def _():
        for c in range(2):
            for k2 in range(RANGE_INNER):
                hs[2 + c, k2 : k2 + 1, :] = filt[c : c + 1, k2 * LANES : (k2 + 1) * LANES]
            hs[c] = hs[2 + c].T
        load(slab)

    @pl.when(step > 0)
    def _():
        load(fresh)

    def rows(p):
        return pl.ds(p, RANGE_OUTER, stride=PITCH)

    def stage1(i, _):
        ps = (2 * i, 2 * i + 1)
        x = jnp.concatenate(
            [
                jnp.concatenate([xs[c, rows(p), :].astype(jnp.bfloat16) for p in ps], axis=1)
                for c in range(2)
            ],
            axis=0,
        )
        y = dot(t1[...], x)
        for k in range(2):
            re, im = y[:LANES, k * LANES : (k + 1) * LANES], y[LANES:, k * LANES : (k + 1) * LANES]
            at = pl.ds(pl.multiple_of((2 * i + k) * LANES, LANES), LANES)
            first[at, :LANES] = (re * w_in[0] - im * w_in[1]).astype(jnp.bfloat16)
            first[at, LANES:] = (re * w_in[1] + im * w_in[0]).astype(jnp.bfloat16)
        return 0

    def stage2(i, _):
        at = pl.ds(pl.multiple_of(2 * i * LANES, 2 * LANES), 2 * LANES)
        y = dot(first[at, :], t2[...])
        for k in range(2):
            re, im = y[k * LANES : (k + 1) * LANES, :LANES], y[k * LANES : (k + 1) * LANES, LANES:]
            at = pl.ds(pl.multiple_of((2 * i + k) * LANES, LANES), LANES)
            second[at, :LANES] = (re * hs[0] - im * hs[1]).astype(jnp.bfloat16)
            second[at, LANES:] = (re * hs[1] + im * hs[0]).astype(jnp.bfloat16)
        return 0

    def stage3(i, _):
        at = pl.ds(pl.multiple_of(2 * i * LANES, 2 * LANES), 2 * LANES)
        y = dot(second[at, :], t3[...])
        for k in range(2):
            re, im = y[k * LANES : (k + 1) * LANES, :LANES], y[k * LANES : (k + 1) * LANES, LANES:]
            cols = slice(k * LANES, (k + 1) * LANES)
            third[i, :LANES, cols] = (re * w_out[0] - im * w_out[1]).astype(jnp.bfloat16)
            third[i, LANES:, cols] = (re * w_out[1] + im * w_out[0]).astype(jnp.bfloat16)
        return 0

    def stage4(i, _):
        y = dot(t4[...], third[i])
        low = lane_ids(LANES) < HALF
        for k in range(2):
            p = 2 * i + k
            re, im = y[:LANES, k * LANES : (k + 1) * LANES], y[LANES:, k * LANES : (k + 1) * LANES]
            os[0, rows(p), :] = jnp.where(low, re, roll_half(im))
            os[1, rows(p), :] = jnp.where(low, roll_half(re), im)
        return 0

    for stage in (stage1, stage2, stage3, stage4):
        lax.fori_loop(0, STEP // 2, stage, 0, unroll=UNROLL)

    def store(n1, _):
        at = pl.ds(pl.multiple_of(n1 * PITCH, 8), STEP)
        out[n1, 0] = os[0, at, :].astype(jnp.bfloat16)
        out[n1, 1] = os[1, at, :].astype(jnp.bfloat16)
        return 0

    lax.fori_loop(0, RANGE_OUTER, store, 0, unroll=8)


def whole(shape):
    return pl.BlockSpec(shape, lambda *_: (0,) * len(shape))


def range_compress(slab, fresh, range_filter):
    tables = (
        left_table(RANGE_OUTER, -1.0),
        right_table(RANGE_INNER, -1.0),
        right_table(RANGE_INNER, 1.0),
        left_table(RANGE_OUTER, 1.0),
    )
    w_in = np.stack(twiddle(RANGE_OUTER, RANGE_INNER, RANGE_BINS, -1.0))
    w_out = np.stack(twiddle(RANGE_OUTER, RANGE_INNER, RANGE_BINS, 1.0))
    square = whole((2 * LANES, 2 * LANES))
    part = whole((2, LANES, LANES))
    out = jax.ShapeDtypeStruct((DEVICES, 2, ROWS, LANES), jnp.bfloat16)
    return pl.pallas_call(
        range_kernel,
        grid=(ROWS // STEP,),
        in_specs=[
            whole((2, STEP, RANGE_BINS)),
            pl.BlockSpec((2, STEP, RANGE_BINS), lambda i: (0, jnp.maximum(i - 1, 0), 0)),
            whole((2, RANGE_BINS)),
            square,
            square,
            square,
            square,
            part,
            part,
        ],
        out_specs=pl.BlockSpec((DEVICES, 2, STEP, LANES), lambda i: (0, 0, i, 0)),
        out_shape=out,
        scratch_shapes=[
            pltpu.VMEM((2, RANGE_OUTER * PITCH, LANES), jnp.float32),
            pltpu.VMEM((2, RANGE_OUTER * PITCH, LANES), jnp.float32),
            pltpu.VMEM((4, LANES, LANES), jnp.float32),
            pltpu.VMEM((STEP * LANES, 2 * LANES), jnp.bfloat16),
            pltpu.VMEM((STEP * LANES, 2 * LANES), jnp.bfloat16),
            pltpu.VMEM((STEP // 2, 2 * LANES, 2 * LANES), jnp.bfloat16),
        ],
        compiler_params=pltpu.CompilerParams(
            dimension_semantics=("arbitrary",), vmem_limit_bytes=RANGE_LIMIT * MIB
        ),
        cost_estimate=pl.CostEstimate(
            flops=4 * 2 * ROWS * RANGE_BINS * 512, bytes_accessed=8 * MIB, transcendentals=0
        ),
        name="range_compress",
    )(slab, fresh, range_filter, *tables, w_in, w_out)


def prepare_kernel(filt, taps, out, wide, fs):
    for c in range(2):
        for kl in range(PULSE_INNER):
            fs[c, kl * PITCH : kl * PITCH + STEP, :] = filt[c, kl].astype(jnp.float32)
    low = lane_ids(PULSE_INNER) < HALF
    for kb in range(STEP):
        for c in range(2):
            value = fs[c, pl.ds(kb, PULSE_INNER, stride=PITCH), :]
            turned = roll_half(value)
            at = slice(kb * PULSE_INNER, (kb + 1) * PULSE_INNER)
            out[0, c, at, :] = jnp.where(low, value, turned).astype(jnp.bfloat16)
            out[1, c, at, :] = jnp.where(low, turned, value).astype(jnp.bfloat16)

    def spread(i, _):
        at = pl.ds(pl.multiple_of(i * STEP, STEP), STEP)
        for j in range(BAND_MAX):
            column = jnp.broadcast_to(taps[at, j : j + 1], (STEP, LANES))
            wide[j, at, :] = column.astype(jnp.bfloat16)
        return 0

    lax.fori_loop(0, PULSE_INNER, spread, 0, unroll=4)


def prepare(azimuth_filter, taps):
    folded = azimuth_filter.reshape(2, PULSE_INNER, PULSE_OUTER, LANES)
    rows = STEP * PULSE_INNER
    return pl.pallas_call(
        prepare_kernel,
        grid=(PULSE_OUTER // STEP,),
        in_specs=[
            pl.BlockSpec((2, PULSE_INNER, STEP, LANES), lambda i: (0, 0, i, 0)),
            pl.BlockSpec((rows, BAND_MAX), lambda i: (i, 0)),
        ],
        out_specs=[
            pl.BlockSpec((2, 2, rows, LANES), lambda i: (0, 0, i, 0)),
            pl.BlockSpec((BAND_MAX, rows, LANES), lambda i: (0, i, 0)),
        ],
        out_shape=[
            jax.ShapeDtypeStruct((2, 2, PULSES, LANES), jnp.bfloat16),
            jax.ShapeDtypeStruct((BAND_MAX, PULSES, LANES), jnp.bfloat16),
        ],
        scratch_shapes=[pltpu.VMEM((2, PULSE_INNER * PITCH, LANES), jnp.float32)],
        compiler_params=pltpu.CompilerParams(
            dimension_semantics=("arbitrary",), vmem_limit_bytes=60 * MIB
        ),
        cost_estimate=pl.CostEstimate(
            flops=8 * PULSES * LANES, bytes_accessed=34 * MIB, transcendentals=0
        ),
        name="prepare",
    )(folded, taps)


def start_all(pairs, sems):
    copies = [pltpu.make_async_copy(a, b, sems.at[i]) for i, (a, b) in enumerate(pairs)]
    for copy in copies:
        copy.start()
    return copies


def forward_kernel(
    half, got_hbm, g1_hbm, t2, filt_hbm, out_hbm, got, g1, filt, out, ps, ts, sems, out_sems
):
    get_got, get_g1, get_filt = start_all(
        ((got_hbm.at[:, half], got), (g1_hbm, g1), (filt_hbm.at[half], filt)), sems
    )
    get_got.wait()
    quarter = PULSE_INNER // STEP
    fresh_units = FRESH_ROWS // STEP

    def unpack(g, _):
        slab = pl.multiple_of(g * INNER_PITCH, 8)
        base = pl.multiple_of((FIRST_OUTER + g * fresh_units) * INNER_PITCH, 8)
        for d in range(quarter):
            block = got[g * quarter + d].astype(jnp.float32)
            ps[pl.ds(slab + d * STEP, STEP), :] = block[:STEP]
            for k in range(fresh_units):
                unit = d * fresh_units + k
                at = base + (unit // quarter) * INNER_PITCH + (unit % quarter) * STEP
                ps[pl.ds(at, STEP), :] = block[(k + 1) * STEP : (k + 2) * STEP]
        return 0

    lax.fori_loop(0, DEVICES // quarter, unpack, 0, unroll=2)

    def outer(l, _):
        x = ps[pl.ds(l, PULSE_OUTER, stride=INNER_PITCH), :]
        both = jnp.concatenate([x.astype(jnp.bfloat16), times_i(x).astype(jnp.bfloat16)], axis=0)
        ts[pl.ds(l, PULSE_OUTER, stride=INNER_PITCH), :] = dot(g1[l], both)
        return 0

    get_g1.wait()
    lax.fori_loop(0, PULSE_INNER, outer, 0, unroll=16)

    def inner(i, _):
        sides = []
        for k in range(2):
            at = pl.ds(pl.multiple_of((2 * i + k) * INNER_PITCH, 8), PULSE_INNER)
            t = ts[at, :]
            sides.append(
                jnp.concatenate([t.astype(jnp.bfloat16), times_i(t).astype(jnp.bfloat16)], axis=0)
            )
        y = dot(t2[...], jnp.concatenate(sides, axis=1))
        for k in range(2):
            at = pl.ds(pl.multiple_of((2 * i + k) * PULSE_INNER, PULSE_INNER), PULSE_INNER)
            cols = slice(k * LANES, (k + 1) * LANES)
            out[at, :] = (
                y[:PULSE_INNER, cols] * filt[0, at, :].astype(jnp.float32)
                + y[PULSE_INNER:, cols] * filt[1, at, :].astype(jnp.float32)
            ).astype(jnp.bfloat16)
        return 0

    get_filt.wait()
    put_in_parts(inner, PULSE_OUTER // 2, 16, out, out_hbm, out_sems)


def put_in_parts(step, count, unroll, source, target, sems):
    rows = source.shape[0] // PARTS
    copies = []
    for i in range(PARTS):
        lax.fori_loop(i * count // PARTS, (i + 1) * count // PARTS, step, 0, unroll=unroll)
        at = pl.ds(i * rows, rows)
        copies.append(pltpu.make_async_copy(source.at[at], target.at[at], sems.at[i]))
        copies[i].start()
    for copy in copies:
        copy.wait()


def azimuth_forward(got, filt, half):
    g1 = turned_tables(PULSE_OUTER, PULSE_INNER, -1.0)
    re, im = dft_table(PULSE_INNER, -1.0)
    t2 = bf16(np.block([[re, im], [-im, re]]))
    return pl.pallas_call(
        functools.partial(forward_kernel, half),
        in_specs=[in_hbm(), in_hbm(), in_vmem(), in_hbm()],
        out_specs=in_hbm(),
        out_shape=jax.ShapeDtypeStruct((PULSES, LANES), jnp.bfloat16),
        scratch_shapes=[
            pltpu.VMEM((DEVICES, ROWS, LANES), jnp.bfloat16),
            pltpu.VMEM(g1.shape, jnp.bfloat16),
            pltpu.VMEM((2, PULSES, LANES), jnp.bfloat16),
            pltpu.VMEM((PULSES, LANES), jnp.bfloat16),
            pltpu.VMEM((PULSE_OUTER * INNER_PITCH, LANES), jnp.float32),
            pltpu.VMEM((PULSE_OUTER * INNER_PITCH, LANES), jnp.float32),
            pltpu.SemaphoreType.DMA((3,)),
            pltpu.SemaphoreType.DMA((PARTS,)),
        ],
        compiler_params=pltpu.CompilerParams(vmem_limit_bytes=FWD_LIMIT * MIB),
        cost_estimate=pl.CostEstimate(
            flops=2 * PULSES * LANES * 512, bytes_accessed=12 * MIB, transcendentals=0
        ),
        name="azimuth_forward",
    )(got, g1, t2, filt)


def inverse_kernel(
    left_hbm,
    right_hbm,
    taps_hbm,
    bands,
    g1_hbm,
    t2,
    by_i,
    out_hbm,
    left,
    right,
    taps,
    g1,
    out,
    sel,
    sums,
    moved,
    vs,
    os,
    sems,
    out_sems,
):
    starts = range(0, BAND_MAX, 2)
    pairs = [(left_hbm, left), (right_hbm, right)]
    for j in starts:
        at = pl.ds(j, min(2, BAND_MAX - j))
        pairs.append((taps_hbm.at[at], taps.at[at]))
    copies = start_all([*pairs, (g1_hbm, g1)], sems)

    index = lax.broadcasted_iota(jnp.int32, (2 * LANES, LANES), 0)
    lane = lax.broadcasted_iota(jnp.int32, (2 * LANES, LANES), 1)
    column = jnp.where(index >= LANES, HALF, 0) + (index & (HALF - 1))
    same = ((index >> 6) & 1) == (lane >> 6)
    want = (lane & (HALF - 1)) + bands[0:1, :]
    for j in range(BAND_MAX):
        hit = same & (column == want + j) & (bands[1:2, :] > j)
        sel[:, j * LANES : (j + 1) * LANES] = jnp.where(hit, 1.0, 0.0).astype(jnp.bfloat16)

    size = GROUP * PULSE_INNER

    def pick(j, g, _):
        at = pl.ds(pl.multiple_of(g * size, size), size)
        wide = min(2, BAND_MAX - j)
        source = jnp.concatenate([left[at, :], right[at, :]], axis=1)
        picked = dot(source, sel[:, j * LANES : (j + wide) * LANES])
        total = None if j == 0 else sums[at, :]
        for k in range(wide):
            weight = taps[j + k, at, :].astype(jnp.float32)
            term = picked[:, k * LANES : (k + 1) * LANES] * weight
            total = term if total is None else total + term
        if j + wide < BAND_MAX:
            sums[at, :] = total
            return 0
        here = total.astype(jnp.bfloat16)
        for k in range(GROUP):
            moved[g * GROUP + k, :PULSE_INNER, :] = here[k * PULSE_INNER : (k + 1) * PULSE_INNER]
        return 0

    def turn(g, _):
        here = [moved[g * GROUP + k, :PULSE_INNER, :] for k in range(GROUP)]
        turned = dot(jnp.concatenate(here, axis=0), by_i[...]).astype(jnp.bfloat16)
        for k in range(GROUP):
            moved[g * GROUP + k, PULSE_INNER:, :] = turned[k * PULSE_INNER : (k + 1) * PULSE_INNER]
        return 0

    copies[0].wait()
    copies[1].wait()
    for j in starts:
        copies[2 + j // 2].wait()
        lax.fori_loop(0, PULSE_OUTER // GROUP, functools.partial(pick, j), 0, unroll=16)
    lax.fori_loop(0, PULSE_OUTER // GROUP, turn, 0, unroll=8)

    def inner(kb, _):
        vs[pl.ds(kb, PULSE_INNER, stride=OUTER_PITCH), :] = dot(g1[kb], moved[kb])
        return 0

    copies[-1].wait()
    lax.fori_loop(0, PULSE_OUTER, inner, 0, unroll=16)

    def last(i, _):
        sides = []
        for k in range(2):
            at = pl.ds(pl.multiple_of((2 * i + k) * OUTER_PITCH, 8), PULSE_OUTER)
            v = vs[at, :]
            sides.append(
                jnp.concatenate([v.astype(jnp.bfloat16), times_i(v).astype(jnp.bfloat16)], axis=0)
            )
        y = dot(t2[...], jnp.concatenate(sides, axis=1))
        for k in range(2):
            os[pl.ds(2 * i + k, KEPT_OUTER, stride=INNER_PITCH), :] = y[
                :, k * LANES : (k + 1) * LANES
            ]
        return 0

    lax.fori_loop(0, PULSE_INNER // 2, last, 0, unroll=8)

    quarter = PULSE_INNER // STEP
    fresh_units = FRESH_ROWS // STEP

    def pack(g, _):
        base = pl.multiple_of(g * fresh_units * INNER_PITCH, 8)
        for d in range(quarter):
            for k in range(fresh_units):
                unit = d * fresh_units + k
                at = (unit // quarter) * INNER_PITCH + (unit % quarter) * STEP
                out[g * quarter + d, k * STEP : (k + 1) * STEP, :] = os[
                    pl.ds(base + at, STEP), :
                ].astype(jnp.bfloat16)
        return 0

    put_in_parts(pack, DEVICES // quarter, 4, out, out_hbm, out_sems)


def azimuth_inverse(left, right, taps, bands):
    g1 = turned_tables(PULSE_INNER, PULSE_OUTER, 1.0)
    re, im = dft_table(PULSE_OUTER, 1.0)
    t2 = bf16(np.concatenate([re[FIRST_OUTER:], im[FIRST_OUTER:]], axis=1))
    return pl.pallas_call(
        inverse_kernel,
        in_specs=[in_hbm()] * 3 + [in_vmem(), in_hbm(), in_vmem(), in_vmem()],
        out_specs=in_hbm(),
        out_shape=jax.ShapeDtypeStruct((DEVICES, FRESH_ROWS, LANES), jnp.bfloat16),
        scratch_shapes=[
            pltpu.VMEM((PULSES, LANES), jnp.bfloat16),
            pltpu.VMEM((PULSES, LANES), jnp.bfloat16),
            pltpu.VMEM((BAND_MAX, PULSES, LANES), jnp.bfloat16),
            pltpu.VMEM(g1.shape, jnp.bfloat16),
            pltpu.VMEM((DEVICES, FRESH_ROWS, LANES), jnp.bfloat16),
            pltpu.VMEM((2 * LANES, BAND_MAX * LANES), jnp.bfloat16),
            pltpu.VMEM((PULSES, LANES), jnp.float32),
            pltpu.VMEM((PULSE_OUTER, 2 * PULSE_INNER, LANES), jnp.bfloat16),
            pltpu.VMEM((PULSE_INNER * OUTER_PITCH, LANES), jnp.float32),
            pltpu.VMEM((KEPT_OUTER * INNER_PITCH, LANES), jnp.float32),
            pltpu.SemaphoreType.DMA((3 + (BAND_MAX + 1) // 2,)),
            pltpu.SemaphoreType.DMA((PARTS,)),
        ],
        compiler_params=pltpu.CompilerParams(vmem_limit_bytes=INV_LIMIT * MIB),
        cost_estimate=pl.CostEstimate(
            flops=2 * PULSES * LANES * (256 * BAND_MAX + 512),
            bytes_accessed=12 * MIB,
            transcendentals=0,
        ),
        name="migrate_inverse",
    )(left, right, taps, bands, g1, t2, turn_table())


def assemble_kernel(first, second, out):
    low = lane_ids(FRESH_ROWS) < HALF

    def one(n1, _):
        a, b = first[n1].astype(jnp.float32), second[n1].astype(jnp.float32)
        at = pl.ds(pl.multiple_of(n1 * LANES, LANES), LANES)
        out[0, :, at] = jnp.where(low, a, roll_half(b)).astype(jnp.bfloat16)
        out[1, :, at] = jnp.where(low, roll_half(a), b).astype(jnp.bfloat16)
        return 0

    lax.fori_loop(0, first.shape[0], one, 0, unroll=16)


def assemble(first, second):
    block = ASSEMBLE
    return pl.pallas_call(
        assemble_kernel,
        grid=(RANGE_OUTER // block,),
        in_specs=[pl.BlockSpec((block, FRESH_ROWS, LANES), lambda i: (i, 0, 0))] * 2,
        out_specs=pl.BlockSpec((2, FRESH_ROWS, block * LANES), lambda i: (0, 0, i)),
        out_shape=jax.ShapeDtypeStruct((2, FRESH_ROWS, RANGE_BINS), jnp.bfloat16),
        compiler_params=pltpu.CompilerParams(
            dimension_semantics=("arbitrary",), vmem_limit_bytes=60 * MIB
        ),
        cost_estimate=pl.CostEstimate(
            flops=4 * FRESH_ROWS * RANGE_BINS, bytes_accessed=6 * MIB, transcendentals=0
        ),
        name="assemble",
    )(first, second)


def exchanged(blocks):
    return lax.all_to_all(blocks, AXES, split_axis=0, concat_axis=0, tiled=True)


def from_next(block):
    size = lax.axis_size(AXES)
    return lax.ppermute(block, AXES, [(i + 1, i) for i in range(size - 1)])


def on_device(
    slab_echoes,
    fresh_pulses,
    range_filter,
    azimuth_filter,
    migration_taps,
    band_offsets,
    band_widths,
):
    got = exchanged(range_compress(slab_echoes, fresh_pulses, range_filter))
    taps = migration_taps.reshape(BAND_MAX, PULSE_INNER, PULSE_OUTER)
    taps = taps.transpose(2, 1, 0).reshape(PULSES, BAND_MAX)
    filt, taps = prepare(azimuth_filter, taps)
    bands = jnp.stack([band_offsets, band_widths]).reshape(2, 2, 1, HALF)
    bands = jnp.broadcast_to(bands, (2, 2, 2, HALF)).reshape(2, 2, LANES)
    spectra0 = azimuth_forward(got, filt, 0)
    rim = from_next(spectra0)
    spectra1 = azimuth_forward(got, filt, 1)
    done0 = exchanged(azimuth_inverse(spectra0, spectra1, taps, bands[:, 0]))
    done1 = exchanged(azimuth_inverse(spectra1, rim, taps, bands[:, 1]))
    return assemble(done0, done1)


def solution(mesh):
    placed = (
        P(None, AXES, None),
        P(None, AXES, None),
        P(),
        P(None, None, AXES),
        P(),
        P(AXES),
        P(AXES),
    )
    return jax.shard_map(
        on_device,
        mesh=mesh,
        in_specs=placed,
        out_specs=P(None, AXES, None),
        check_vma=False,
    )
```

```python
import functools
import math

import jax
import jax.numpy as jnp
import ml_dtypes
import numpy as np
from jax import lax
from jax.experimental import pallas as pl
from jax.experimental.pallas import tpu as pltpu
from jax.sharding import PartitionSpec as P

RANGE_OUTER = 128
RANGE_INNER = 128
PULSE_OUTER = 128
PULSE_INNER = 64
SLAB_PULSES = 2048
BAND_MAX = 9
RANGE_BINS = 16384
PULSES = 8192
FRESH_COUNT = 6144
LANES = 128
HALF = 64
DEVICES = 128
SLAB_ROWS = SLAB_PULSES // DEVICES
FRESH_ROWS = FRESH_COUNT // DEVICES
ROWS = SLAB_ROWS + FRESH_ROWS
STEP = 16
FIRST_OUTER = SLAB_PULSES // PULSE_INNER
KEPT_OUTER = PULSE_OUTER - FIRST_OUTER
GROUP = 4
UNROLL = 8
PITCH = STEP + 4
INNER_PITCH = PULSE_INNER + 8
OUTER_PITCH = PULSE_OUTER + 8
BLOCKS = ROWS // STEP
RANGE_LIMIT = 60
FWD_LIMIT = 60
INV_LIMIT = 60
PARTS = 4
SPREAD = 6
AXES = ("az", "rg")
MIB = 1024 * 1024


def bf16(values):
    return np.asarray(values, np.float32).astype(ml_dtypes.bfloat16)


def dft_table(length, sign):
    index = np.arange(length)
    angle = (np.outer(index, index) % length).astype(np.float32) * np.float32(
        2.0 * math.pi / length
    )
    scale = np.float32(1.0 / math.sqrt(length))
    real_part = bf16(np.cos(angle) * scale).astype(np.float32)
    imag_part = bf16(sign * np.sin(angle) * scale).astype(np.float32)
    return real_part, imag_part


def twiddle(rows_size, cols_size, total, sign):
    angle = (np.outer(np.arange(rows_size), np.arange(cols_size)) % total).astype(
        np.float32
    ) * np.float32(2.0 * math.pi / total)
    return np.cos(angle), np.float32(sign) * np.sin(angle)


def left_table(length, sign):
    re, im = dft_table(length, sign)
    return bf16(np.block([[re, -im], [im, re]]))


def right_table(length, sign):
    re, im = dft_table(length, sign)
    return bf16(np.block([[re, im], [-im, re]]))


def turned_tables(outer, inner, sign):
    re, im = dft_table(outer, sign)
    tw_re, tw_im = twiddle(outer, inner, PULSES, sign)
    turn_re, turn_im = tw_re.T[:, :, None], tw_im.T[:, :, None]
    return bf16(
        np.concatenate(
            [re * turn_re - im * turn_im, re * turn_im + im * turn_re], axis=2
        )
    )


def roll_half(values):
    return pltpu.roll(values, HALF, 1)


def lane_ids(rows):
    return lax.broadcasted_iota(jnp.int32, (rows, LANES), 1)


def times_i(values):
    turned = roll_half(values)
    return jnp.where(lane_ids(values.shape[0]) < HALF, -turned, turned)


def with_i(values):
    return jnp.concatenate([values, times_i(values)], axis=0)


def dot(left, right):
    return jnp.dot(left, right, preferred_element_type=jnp.float32)


def in_vmem():
    return pl.BlockSpec(memory_space=pltpu.VMEM)


def in_hbm():
    return pl.BlockSpec(memory_space=pl.ANY)


def range_kernel(slab, fresh, filt, t1, t2, t3, t4, w_in, w_out, out, xs, os, hs, first, second, third):
    step = pl.program_id(0)

    def load(source):
        def one(n1, _):
            at = pl.ds(pl.multiple_of(n1 * LANES, LANES), LANES)
            to = pl.ds(pl.multiple_of(n1 * PITCH, 4), STEP)
            for c in range(2):
                xs[c, to, :] = source[c, :, at].astype(jnp.float32)
            return 0

        lax.fori_loop(0, RANGE_OUTER, one, 0, unroll=8)

    @pl.when(step == 0)
    def _():
        for c in range(2):
            for k2 in range(RANGE_INNER):
                hs[2 + c, k2 : k2 + 1, :] = filt[c : c + 1, k2 * LANES : (k2 + 1) * LANES]
            hs[c] = hs[2 + c].T
        load(slab)

    @pl.when(step > 0)
    def _():
        load(fresh)

    def rows(p):
        return pl.ds(p, RANGE_OUTER, stride=PITCH)

    def stage1(i, _):
        ps = (2 * i, 2 * i + 1)
        x = jnp.concatenate(
            [
                jnp.concatenate([xs[c, rows(p), :].astype(jnp.bfloat16) for p in ps], axis=1)
                for c in range(2)
            ],
            axis=0,
        )
        y = dot(t1[...], x)
        for k in range(2):
            re, im = y[:LANES, k * LANES : (k + 1) * LANES], y[LANES:, k * LANES : (k + 1) * LANES]
            at = pl.ds(pl.multiple_of((2 * i + k) * LANES, LANES), LANES)
            first[at, :LANES] = (re * w_in[0] - im * w_in[1]).astype(jnp.bfloat16)
            first[at, LANES:] = (re * w_in[1] + im * w_in[0]).astype(jnp.bfloat16)
        return 0

    def stage2(i, _):
        at = pl.ds(pl.multiple_of(2 * i * LANES, 2 * LANES), 2 * LANES)
        y = dot(first[at, :], t2[...])
        for k in range(2):
            re, im = y[k * LANES : (k + 1) * LANES, :LANES], y[k * LANES : (k + 1) * LANES, LANES:]
            at = pl.ds(pl.multiple_of((2 * i + k) * LANES, LANES), LANES)
            second[at, :LANES] = (re * hs[0] - im * hs[1]).astype(jnp.bfloat16)
            second[at, LANES:] = (re * hs[1] + im * hs[0]).astype(jnp.bfloat16)
        return 0

    def stage3(i, _):
        at = pl.ds(pl.multiple_of(2 * i * LANES, 2 * LANES), 2 * LANES)
        y = dot(second[at, :], t3[...])
        for k in range(2):
            re, im = y[k * LANES : (k + 1) * LANES, :LANES], y[k * LANES : (k + 1) * LANES, LANES:]
            cols = slice(k * LANES, (k + 1) * LANES)
            third[i, :LANES, cols] = (re * w_out[0] - im * w_out[1]).astype(jnp.bfloat16)
            third[i, LANES:, cols] = (re * w_out[1] + im * w_out[0]).astype(jnp.bfloat16)
        return 0

    def stage4(i, _):
        y = dot(t4[...], third[i])
        low = lane_ids(LANES) < HALF
        for k in range(2):
            p = 2 * i + k
            re, im = y[:LANES, k * LANES : (k + 1) * LANES], y[LANES:, k * LANES : (k + 1) * LANES]
            os[0, rows(p), :] = jnp.where(low, re, roll_half(im))
            os[1, rows(p), :] = jnp.where(low, roll_half(re), im)
        return 0

    for stage in (stage1, stage2, stage3, stage4):
        lax.fori_loop(0, STEP // 2, stage, 0, unroll=UNROLL)

    def store(n1, _):
        at = pl.ds(pl.multiple_of(n1 * PITCH, 4), STEP)
        out[n1, 0] = os[0, at, :].astype(jnp.bfloat16)
        out[n1, 1] = os[1, at, :].astype(jnp.bfloat16)
        return 0

    lax.fori_loop(0, RANGE_OUTER, store, 0, unroll=8)


def whole(shape):
    return pl.BlockSpec(shape, lambda *_: (0,) * len(shape))


def range_compress(slab, fresh, range_filter):
    tables = (
        left_table(RANGE_OUTER, -1.0),
        right_table(RANGE_INNER, -1.0),
        right_table(RANGE_INNER, 1.0),
        left_table(RANGE_OUTER, 1.0),
    )
    w_in = np.stack(twiddle(RANGE_OUTER, RANGE_INNER, RANGE_BINS, -1.0))
    w_out = np.stack(twiddle(RANGE_OUTER, RANGE_INNER, RANGE_BINS, 1.0))
    square = whole((2 * LANES, 2 * LANES))
    part = whole((2, LANES, LANES))
    out = jax.ShapeDtypeStruct((DEVICES, 2, ROWS, LANES), jnp.bfloat16)
    return pl.pallas_call(
        range_kernel,
        grid=(ROWS // STEP,),
        in_specs=[
            whole((2, STEP, RANGE_BINS)),
            pl.BlockSpec((2, STEP, RANGE_BINS), lambda i: (0, jnp.maximum(i - 1, 0), 0)),
            whole((2, RANGE_BINS)),
            square,
            square,
            square,
            square,
            part,
            part,
        ],
        out_specs=pl.BlockSpec((DEVICES, 2, STEP, LANES), lambda i: (0, 0, i, 0)),
        out_shape=out,
        scratch_shapes=[
            pltpu.VMEM((2, RANGE_OUTER * PITCH, LANES), jnp.float32),
            pltpu.VMEM((2, RANGE_OUTER * PITCH, LANES), jnp.float32),
            pltpu.VMEM((4, LANES, LANES), jnp.float32),
            pltpu.VMEM((STEP * LANES, 2 * LANES), jnp.bfloat16),
            pltpu.VMEM((STEP * LANES, 2 * LANES), jnp.bfloat16),
            pltpu.VMEM((STEP // 2, 2 * LANES, 2 * LANES), jnp.bfloat16),
        ],
        compiler_params=pltpu.CompilerParams(
            dimension_semantics=("arbitrary",), vmem_limit_bytes=RANGE_LIMIT * MIB
        ),
        cost_estimate=pl.CostEstimate(
            flops=4 * 2 * ROWS * RANGE_BINS * 512, bytes_accessed=8 * MIB, transcendentals=0
        ),
        name="range_compress",
    )(slab, fresh, range_filter, *tables, w_in, w_out)


def prepare_kernel(filt, taps, out, narrow, wide, fs):
    narrow[:, :BAND_MAX] = taps[...].astype(jnp.bfloat16)
    for c in range(2):
        for kl in range(PULSE_INNER):
            fs[c, kl * PITCH : kl * PITCH + STEP, :] = filt[c, kl].astype(jnp.float32)
    low = lane_ids(PULSE_INNER) < HALF
    for kb in range(STEP):
        for c in range(2):
            value = fs[c, pl.ds(kb, PULSE_INNER, stride=PITCH), :]
            turned = roll_half(value)
            at = slice(kb * PULSE_INNER, (kb + 1) * PULSE_INNER)
            out[0, c, at, :] = jnp.where(low, value, turned).astype(jnp.bfloat16)
            out[1, c, at, :] = jnp.where(low, turned, value).astype(jnp.bfloat16)

    def spread(i, _):
        at = pl.ds(pl.multiple_of(i * STEP, STEP), STEP)
        for j in range(SPREAD):
            column = jnp.broadcast_to(taps[at, j : j + 1], (STEP, LANES))
            wide[j, at, :] = column.astype(jnp.bfloat16)
        return 0

    lax.fori_loop(0, PULSE_INNER, spread, 0, unroll=4)


def prepare(azimuth_filter, taps):
    folded = azimuth_filter.reshape(2, PULSE_INNER, PULSE_OUTER, LANES)
    rows = STEP * PULSE_INNER
    return pl.pallas_call(
        prepare_kernel,
        grid=(PULSE_OUTER // STEP,),
        in_specs=[
            pl.BlockSpec((2, PULSE_INNER, STEP, LANES), lambda i: (0, 0, i, 0)),
            pl.BlockSpec((rows, BAND_MAX), lambda i: (i, 0)),
        ],
        out_specs=[
            pl.BlockSpec((2, 2, rows, LANES), lambda i: (0, 0, i, 0)),
            pl.BlockSpec((rows, LANES), lambda i: (i, 0)),
            pl.BlockSpec((SPREAD, rows, LANES), lambda i: (0, i, 0)),
        ],
        out_shape=[
            jax.ShapeDtypeStruct((2, 2, PULSES, LANES), jnp.bfloat16),
            jax.ShapeDtypeStruct((PULSES, LANES), jnp.bfloat16),
            jax.ShapeDtypeStruct((SPREAD, PULSES, LANES), jnp.bfloat16),
        ],
        scratch_shapes=[pltpu.VMEM((2, PULSE_INNER * PITCH, LANES), jnp.float32)],
        compiler_params=pltpu.CompilerParams(
            dimension_semantics=("arbitrary",), vmem_limit_bytes=60 * MIB
        ),
        cost_estimate=pl.CostEstimate(
            flops=8 * PULSES * LANES, bytes_accessed=34 * MIB, transcendentals=0
        ),
        name="prepare",
    )(folded, taps)


def start_all(pairs, sems):
    copies = [pltpu.make_async_copy(a, b, sems.at[i]) for i, (a, b) in enumerate(pairs)]
    for copy in copies:
        copy.start()
    return copies


def then_start(copy, others):
    def run():
        copy.wait()
        for other in others:
            other.start()

    return run


def forward_steps(got, g1, t2, filt, out, ps, ts, waits):
    waits[0]()
    quarter = PULSE_INNER // STEP
    fresh_units = FRESH_ROWS // STEP

    def unpack(g, _):
        slab = pl.multiple_of(g * INNER_PITCH, 8)
        base = pl.multiple_of((FIRST_OUTER + g * fresh_units) * INNER_PITCH, 8)
        for d in range(quarter):
            block = got[g * quarter + d].astype(jnp.float32)
            ps[pl.ds(slab + d * STEP, STEP), :] = block[:STEP]
            for k in range(fresh_units):
                unit = d * fresh_units + k
                at = base + (unit // quarter) * INNER_PITCH + (unit % quarter) * STEP
                ps[pl.ds(at, STEP), :] = block[(k + 1) * STEP : (k + 2) * STEP]
        return 0

    lax.fori_loop(0, DEVICES // quarter, unpack, 0, unroll=2)

    def outer(l, _):
        x = ps[pl.ds(l, PULSE_OUTER, stride=INNER_PITCH), :]
        both = with_i(x.astype(jnp.bfloat16))
        ts[pl.ds(l, PULSE_OUTER, stride=INNER_PITCH), :] = dot(g1[l], both)
        return 0

    waits[1]()
    lax.fori_loop(0, PULSE_INNER, outer, 0, unroll=16)

    def inner(i, _):
        sides = []
        for k in range(2):
            at = pl.ds(pl.multiple_of((2 * i + k) * INNER_PITCH, 8), PULSE_INNER)
            t = ts[at, :]
            sides.append(
                with_i(t.astype(jnp.bfloat16))
            )
        y = dot(t2[...], jnp.concatenate(sides, axis=1))
        for k in range(2):
            at = pl.ds(pl.multiple_of((2 * i + k) * PULSE_INNER, PULSE_INNER), PULSE_INNER)
            cols = slice(k * LANES, (k + 1) * LANES)
            out[at, :] = (
                y[:PULSE_INNER, cols] * filt[0, at, :].astype(jnp.float32)
                + y[PULSE_INNER:, cols] * filt[1, at, :].astype(jnp.float32)
            ).astype(jnp.bfloat16)
        return 0

    waits[2]()
    return inner


def forward_kernel(
    half, got_hbm, g1_hbm, t2, filt_hbm, out_hbm, got, g1, filt, out, ps, ts, sems, out_sems
):
    copies = start_all(((got_hbm.at[:, half], got), (g1_hbm, g1)), sems)
    last = pltpu.make_async_copy(filt_hbm.at[half], filt, sems.at[2])
    waits = [then_start(copies[0], [last]), copies[1].wait, last.wait]
    inner = forward_steps(got, g1, t2, filt, out, ps, ts, waits)
    put_in_parts(inner, PULSE_OUTER // 2, 16, out, out_hbm, out_sems)


def put_in_parts(step, count, unroll, source, target, sems):
    rows = source.shape[0] // PARTS
    copies = []
    for i in range(PARTS):
        lax.fori_loop(i * count // PARTS, (i + 1) * count // PARTS, step, 0, unroll=unroll)
        at = pl.ds(i * rows, rows)
        copies.append(pltpu.make_async_copy(source.at[at], target.at[at], sems.at[i]))
        copies[i].start()
    for copy in copies:
        copy.wait()


def azimuth_forward(got, filt, half):
    g1, t2 = forward_tables()
    return pl.pallas_call(
        functools.partial(forward_kernel, half),
        in_specs=[in_hbm(), in_hbm(), in_vmem(), in_hbm()],
        out_specs=in_hbm(),
        out_shape=jax.ShapeDtypeStruct((PULSES, LANES), jnp.bfloat16),
        scratch_shapes=[
            pltpu.VMEM((DEVICES, ROWS, LANES), jnp.bfloat16),
            pltpu.VMEM(g1.shape, jnp.bfloat16),
            pltpu.VMEM((2, PULSES, LANES), jnp.bfloat16),
            pltpu.VMEM((PULSES, LANES), jnp.bfloat16),
            pltpu.VMEM((PULSE_OUTER * INNER_PITCH, LANES), jnp.float32),
            pltpu.VMEM((PULSE_OUTER * INNER_PITCH, LANES), jnp.float32),
            pltpu.SemaphoreType.DMA((3,)),
            pltpu.SemaphoreType.DMA((PARTS,)),
        ],
        compiler_params=pltpu.CompilerParams(vmem_limit_bytes=FWD_LIMIT * MIB),
        cost_estimate=pl.CostEstimate(
            flops=2 * PULSES * LANES * 512, bytes_accessed=12 * MIB, transcendentals=0
        ),
        name="azimuth_forward",
    )(got, g1, t2, filt)


def tap_steps():
    later = [(j, min(2, BAND_MAX - j)) for j in range(SPREAD, BAND_MAX, 2)]
    return later + [(j, 2) for j in range(0, SPREAD, 2)]


def tap_pairs(narrow_hbm, narrow, taps_hbm, taps):
    spans = [pl.ds(j, 2) for j in range(0, SPREAD, 2)]
    return [(narrow_hbm, narrow)] + [(taps_hbm.at[at], taps.at[at]) for at in spans]


def select_table(half, bands, sel):
    index = lax.broadcasted_iota(jnp.int32, (2 * LANES, LANES), 0)
    lane = lax.broadcasted_iota(jnp.int32, (2 * LANES, LANES), 1)
    column = jnp.where(index >= LANES, HALF, 0) + (index & (HALF - 1))
    same = ((index >> 6) & 1) == (lane >> 6)
    want = (lane & (HALF - 1)) + bands[half : half + 1, :]
    for j in range(BAND_MAX):
        hit = same & (column == want + j) & (bands[2 + half : 3 + half, :] > j)
        sel[:, j * LANES : (j + 1) * LANES] = jnp.where(hit, 1.0, 0.0).astype(jnp.bfloat16)


def inverse_steps(
    left, right, narrow, taps, sel, g1, t2, out, out_hbm, sums, moved, vs, os, waits, out_sems
):
    size = GROUP * PULSE_INNER

    steps = tap_steps()

    def pick(order, g, _):
        j, wide = steps[order]
        at = pl.ds(pl.multiple_of(g * size, size), size)
        source = jnp.concatenate([left[at, :], right[at, :]], axis=1)
        picked = dot(source, sel[:, j * LANES : (j + wide) * LANES])
        total = None if order == 0 else sums[at, :]
        if j >= SPREAD:
            columns = narrow[at, :].astype(jnp.float32)
        for k in range(wide):
            if j >= SPREAD:
                weight = columns[:, j + k : j + k + 1]
            else:
                weight = taps[j + k, at, :].astype(jnp.float32)
            term = picked[:, k * LANES : (k + 1) * LANES] * weight
            total = term if total is None else total + term
        if order + 1 < len(steps):
            sums[at, :] = total
        else:
            moved[at, :] = total.astype(jnp.bfloat16)
        return 0

    waits[0]()
    waits[1]()
    for order, (j, _) in enumerate(steps):
        if j < SPREAD:
            waits[2 + j // 2]()
        lax.fori_loop(0, PULSE_OUTER // GROUP, functools.partial(pick, order), 0, unroll=32)

    def inner(kb, _):
        at = pl.ds(pl.multiple_of(kb * PULSE_INNER, PULSE_INNER), PULSE_INNER)
        vs[pl.ds(kb, PULSE_INNER, stride=OUTER_PITCH), :] = dot(g1[kb], with_i(moved[at, :]))
        return 0

    waits[-1]()
    lax.fori_loop(0, PULSE_OUTER, inner, 0, unroll=32)

    def last(i, _):
        sides = []
        for k in range(2):
            at = pl.ds(pl.multiple_of((2 * i + k) * OUTER_PITCH, 8), PULSE_OUTER)
            v = vs[at, :]
            sides.append(
                with_i(v.astype(jnp.bfloat16))
            )
        y = dot(t2[...], jnp.concatenate(sides, axis=1))
        for k in range(2):
            os[pl.ds(2 * i + k, KEPT_OUTER, stride=INNER_PITCH), :] = y[
                :, k * LANES : (k + 1) * LANES
            ]
        return 0

    lax.fori_loop(0, PULSE_INNER // 2, last, 0, unroll=8)

    quarter = PULSE_INNER // STEP
    fresh_units = FRESH_ROWS // STEP

    def pack(g, _):
        base = pl.multiple_of(g * fresh_units * INNER_PITCH, 8)
        for d in range(quarter):
            for k in range(fresh_units):
                unit = d * fresh_units + k
                at = (unit // quarter) * INNER_PITCH + (unit % quarter) * STEP
                out[g * quarter + d, k * STEP : (k + 1) * STEP, :] = os[
                    pl.ds(base + at, STEP), :
                ].astype(jnp.bfloat16)
        return 0

    put_in_parts(pack, DEVICES // quarter, 4, out, out_hbm, out_sems)


def inverse_kernel(
    left_hbm,
    right_hbm,
    narrow_hbm,
    taps_hbm,
    bands,
    g1_hbm,
    t2,
    out_hbm,
    left,
    right,
    narrow,
    taps,
    g1,
    out,
    sel,
    sums,
    moved,
    vs,
    os,
    sems,
    out_sems,
):
    pairs = [(left_hbm, left), (right_hbm, right), *tap_pairs(narrow_hbm, narrow, taps_hbm, taps), (g1_hbm, g1)]
    copies = start_all(pairs, sems)
    select_table(1, bands, sel)

    def both():
        copies[0].wait()
        copies[1].wait()

    waits = [both, *[copy.wait for copy in copies[2:]]]
    inverse_steps(
        left, right, narrow, taps, sel, g1, t2, out, out_hbm, sums, moved, vs, os, waits, out_sems
    )


def middle_kernel(
    half,
    got_hbm,
    f1_hbm,
    f2,
    filt_hbm,
    left_hbm,
    narrow_hbm,
    taps_hbm,
    bands,
    g1_hbm,
    t2,
    right_hbm,
    out_hbm,
    got,
    f1,
    filt,
    right,
    ps,
    ts,
    left,
    narrow,
    taps,
    g1,
    out,
    sel,
    sums,
    moved,
    sems,
    late_sems,
    right_sem,
    out_sems,
):
    first = start_all(((got_hbm.at[:, half], got), (f1_hbm, f1)), sems)
    first.append(pltpu.make_async_copy(filt_hbm.at[half], filt, sems.at[2]))
    pairs = [(left_hbm, left), *tap_pairs(narrow_hbm, narrow, taps_hbm, taps), (g1_hbm, g1)]
    late = [pltpu.make_async_copy(a, b, late_sems.at[i]) for i, (a, b) in enumerate(pairs)]
    select_table(0, bands, sel)

    cut = 4
    waits = [
        then_start(first[0], first[2:]),
        then_start(first[1], late[:cut]),
        then_start(first[2], late[cut:]),
    ]
    inner = forward_steps(got, f1, f2, filt, right, ps, ts, waits)
    lax.fori_loop(0, PULSE_OUTER // 2, inner, 0, unroll=16)
    put_right = pltpu.make_async_copy(right, right_hbm, right_sem.at[0])
    put_right.start()
    waits = [copy.wait for copy in late]
    inverse_steps(
        left, right, narrow, taps, sel, g1, t2, out, out_hbm, sums, moved, ts, ps, waits, out_sems
    )
    put_right.wait()


def forward_tables():
    re, im = dft_table(PULSE_INNER, -1.0)
    t2 = bf16(np.block([[re, im], [-im, re]]))
    return turned_tables(PULSE_OUTER, PULSE_INNER, -1.0), t2


def inverse_tables():
    re, im = dft_table(PULSE_OUTER, 1.0)
    t2 = bf16(np.concatenate([re[FIRST_OUTER:], im[FIRST_OUTER:]], axis=1))
    return turned_tables(PULSE_INNER, PULSE_OUTER, 1.0), t2


def forward_and_inverse(got, filt, half, left, narrow, taps, bands):
    f1, f2 = forward_tables()
    g1, t2 = inverse_tables()
    return pl.pallas_call(
        functools.partial(middle_kernel, half),
        in_specs=[in_hbm(), in_hbm(), in_vmem()] + [in_hbm()] * 4
        + [in_vmem(), in_hbm(), in_vmem()],
        out_specs=[in_hbm(), in_hbm()],
        out_shape=[
            jax.ShapeDtypeStruct((PULSES, LANES), jnp.bfloat16),
            jax.ShapeDtypeStruct((DEVICES, FRESH_ROWS, LANES), jnp.bfloat16),
        ],
        scratch_shapes=[
            pltpu.VMEM((DEVICES, ROWS, LANES), jnp.bfloat16),
            pltpu.VMEM(f1.shape, jnp.bfloat16),
            pltpu.VMEM((2, PULSES, LANES), jnp.bfloat16),
            pltpu.VMEM((PULSES, LANES), jnp.bfloat16),
            pltpu.VMEM((PULSE_OUTER * INNER_PITCH, LANES), jnp.float32),
            pltpu.VMEM((PULSE_OUTER * INNER_PITCH, LANES), jnp.float32),
            pltpu.VMEM((PULSES, LANES), jnp.bfloat16),
            pltpu.VMEM((PULSES, LANES), jnp.bfloat16),
            pltpu.VMEM((SPREAD, PULSES, LANES), jnp.bfloat16),
            pltpu.VMEM(g1.shape, jnp.bfloat16),
            pltpu.VMEM((DEVICES, FRESH_ROWS, LANES), jnp.bfloat16),
            pltpu.VMEM((2 * LANES, BAND_MAX * LANES), jnp.bfloat16),
            pltpu.VMEM((PULSES, LANES), jnp.float32),
            pltpu.VMEM((PULSES, LANES), jnp.bfloat16),
            pltpu.SemaphoreType.DMA((3,)),
            pltpu.SemaphoreType.DMA((3 + SPREAD // 2,)),
            pltpu.SemaphoreType.DMA((1,)),
            pltpu.SemaphoreType.DMA((PARTS,)),
        ],
        compiler_params=pltpu.CompilerParams(vmem_limit_bytes=INV_LIMIT * MIB),
        cost_estimate=pl.CostEstimate(
            flops=2 * PULSES * LANES * (256 * BAND_MAX + 1024),
            bytes_accessed=40 * MIB,
            transcendentals=0,
        ),
        name="forward_inverse",
    )(got, f1, f2, filt, left, narrow, taps, bands, g1, t2)


def azimuth_inverse(left, right, narrow, taps, bands):
    g1, t2 = inverse_tables()
    return pl.pallas_call(
        inverse_kernel,
        in_specs=[in_hbm()] * 4 + [in_vmem(), in_hbm(), in_vmem()],
        out_specs=in_hbm(),
        out_shape=jax.ShapeDtypeStruct((DEVICES, FRESH_ROWS, LANES), jnp.bfloat16),
        scratch_shapes=[
            pltpu.VMEM((PULSES, LANES), jnp.bfloat16),
            pltpu.VMEM((PULSES, LANES), jnp.bfloat16),
            pltpu.VMEM((PULSES, LANES), jnp.bfloat16),
            pltpu.VMEM((SPREAD, PULSES, LANES), jnp.bfloat16),
            pltpu.VMEM(g1.shape, jnp.bfloat16),
            pltpu.VMEM((DEVICES, FRESH_ROWS, LANES), jnp.bfloat16),
            pltpu.VMEM((2 * LANES, BAND_MAX * LANES), jnp.bfloat16),
            pltpu.VMEM((PULSES, LANES), jnp.float32),
            pltpu.VMEM((PULSES, LANES), jnp.bfloat16),
            pltpu.VMEM((PULSE_INNER * OUTER_PITCH, LANES), jnp.float32),
            pltpu.VMEM((KEPT_OUTER * INNER_PITCH, LANES), jnp.float32),
            pltpu.SemaphoreType.DMA((4 + SPREAD // 2,)),
            pltpu.SemaphoreType.DMA((PARTS,)),
        ],
        compiler_params=pltpu.CompilerParams(vmem_limit_bytes=INV_LIMIT * MIB),
        cost_estimate=pl.CostEstimate(
            flops=2 * PULSES * LANES * (256 * BAND_MAX + 512),
            bytes_accessed=12 * MIB,
            transcendentals=0,
        ),
        name="migrate_inverse",
    )(left, right, narrow, taps, bands, g1, t2)


def assemble_kernel(first_hbm, second_hbm, out_hbm, first, second, out, sems, more_sems, out_sems):
    low = lane_ids(FRESH_ROWS) < HALF
    size = RANGE_OUTER // PARTS
    spans = [pl.ds(i * size, size) for i in range(PARTS)]
    copies = start_all([(first_hbm.at[at], first.at[at]) for at in spans], sems)
    more = start_all([(second_hbm.at[at], second.at[at]) for at in spans], more_sems)

    def one(n1, _):
        a, b = first[n1].astype(jnp.float32), second[n1].astype(jnp.float32)
        at = pl.ds(pl.multiple_of(n1 * LANES, LANES), LANES)
        out[0, :, at] = jnp.where(low, a, roll_half(b)).astype(jnp.bfloat16)
        out[1, :, at] = jnp.where(low, roll_half(a), b).astype(jnp.bfloat16)
        return 0

    puts = []
    for i in range(PARTS):
        copies[i].wait()
        more[i].wait()
        lax.fori_loop(i * size, (i + 1) * size, one, 0, unroll=16)
        at = pl.ds(i * size * LANES, size * LANES)
        puts.append(pltpu.make_async_copy(out.at[:, :, at], out_hbm.at[:, :, at], out_sems.at[i]))
        puts[i].start()
    for put in puts:
        put.wait()


def assemble(first, second):
    part = pltpu.VMEM((RANGE_OUTER, FRESH_ROWS, LANES), jnp.bfloat16)
    shape = (2, FRESH_ROWS, RANGE_BINS)
    return pl.pallas_call(
        assemble_kernel,
        in_specs=[in_hbm(), in_hbm()],
        out_specs=in_hbm(),
        out_shape=jax.ShapeDtypeStruct(shape, jnp.bfloat16),
        scratch_shapes=[
            part,
            part,
            pltpu.VMEM(shape, jnp.bfloat16),
            pltpu.SemaphoreType.DMA((PARTS,)),
            pltpu.SemaphoreType.DMA((PARTS,)),
            pltpu.SemaphoreType.DMA((PARTS,)),
        ],
        compiler_params=pltpu.CompilerParams(vmem_limit_bytes=60 * MIB),
        cost_estimate=pl.CostEstimate(
            flops=4 * FRESH_ROWS * RANGE_BINS, bytes_accessed=6 * MIB, transcendentals=0
        ),
        name="assemble",
    )(first, second)


def exchanged(blocks):
    return lax.all_to_all(blocks, AXES, split_axis=0, concat_axis=0, tiled=True)


def from_next(block):
    size = lax.axis_size(AXES)
    return lax.ppermute(block, AXES, [(i + 1, i) for i in range(size - 1)])


def on_device(
    slab_echoes,
    fresh_pulses,
    range_filter,
    azimuth_filter,
    migration_taps,
    band_offsets,
    band_widths,
):
    got = exchanged(range_compress(slab_echoes, fresh_pulses, range_filter))
    taps = migration_taps.reshape(BAND_MAX, PULSE_INNER, PULSE_OUTER)
    taps = taps.transpose(2, 1, 0).reshape(PULSES, BAND_MAX)
    filt, narrow, taps = prepare(azimuth_filter, taps)
    bands = jnp.stack([band_offsets, band_widths]).reshape(2, 2, 1, HALF)
    bands = jnp.broadcast_to(bands, (2, 2, 2, HALF)).reshape(4, LANES)
    spectra0 = azimuth_forward(got, filt, 0)
    rim = from_next(spectra0)
    spectra1, ready0 = forward_and_inverse(got, filt, 1, spectra0, narrow, taps, bands)
    done0 = exchanged(ready0)
    done1 = exchanged(azimuth_inverse(spectra1, rim, narrow, taps, bands))
    return assemble(done0, done1)


def solution(mesh):
    placed = (
        P(None, AXES, None),
        P(None, AXES, None),
        P(),
        P(None, None, AXES),
        P(),
        P(AXES),
        P(AXES),
    )
    return jax.shard_map(
        on_device,
        mesh=mesh,
        in_specs=placed,
        out_specs=P(None, AXES, None),
        check_vma=False,
    )
```

```python
import functools
import math

import jax
import jax.numpy as jnp
import ml_dtypes
import numpy as np
from jax import lax
from jax.experimental import pallas as pl
from jax.experimental.pallas import tpu as pltpu
from jax.sharding import PartitionSpec as P

RANGE_OUTER = 128
RANGE_INNER = 128
PULSE_OUTER = 128
PULSE_INNER = 64
SLAB_PULSES = 2048
BAND_MAX = 9
RANGE_BINS = 16384
PULSES = 8192
FRESH_COUNT = 6144
LANES = 128
HALF = 64
DEVICES = 128
SLAB_ROWS = SLAB_PULSES // DEVICES
FRESH_ROWS = FRESH_COUNT // DEVICES
ROWS = SLAB_ROWS + FRESH_ROWS
STEP = 16
FIRST_OUTER = SLAB_PULSES // PULSE_INNER
KEPT_OUTER = PULSE_OUTER - FIRST_OUTER
GROUP = 4
UNROLL = 8
PITCH = STEP + 4
INNER_PITCH = PULSE_INNER + 8
OUTER_PITCH = PULSE_OUTER + 8
SPARE = 128
BLOCKS = ROWS // STEP
RANGE_LIMIT = 60
FWD_LIMIT = 60
INV_LIMIT = 60
PARTS = 4
SPREAD = 6
AXES = ("az", "rg")
MIB = 1024 * 1024


def bf16(values):
    return np.asarray(values, np.float32).astype(ml_dtypes.bfloat16)


def dft_table(length, sign):
    index = np.arange(length)
    angle = (np.outer(index, index) % length).astype(np.float32) * np.float32(
        2.0 * math.pi / length
    )
    scale = np.float32(1.0 / math.sqrt(length))
    real_part = bf16(np.cos(angle) * scale).astype(np.float32)
    imag_part = bf16(sign * np.sin(angle) * scale).astype(np.float32)
    return real_part, imag_part


def twiddle(rows_size, cols_size, total, sign):
    angle = (np.outer(np.arange(rows_size), np.arange(cols_size)) % total).astype(
        np.float32
    ) * np.float32(2.0 * math.pi / total)
    return np.cos(angle), np.float32(sign) * np.sin(angle)


def left_table(length, sign):
    re, im = dft_table(length, sign)
    return bf16(np.block([[re, -im], [im, re]]))


def right_table(length, sign):
    re, im = dft_table(length, sign)
    return bf16(np.block([[re, im], [-im, re]]))


def turned_tables(outer, inner, sign):
    re, im = dft_table(outer, sign)
    tw_re, tw_im = twiddle(outer, inner, PULSES, sign)
    turn_re, turn_im = tw_re.T[:, :, None], tw_im.T[:, :, None]
    return bf16(
        np.concatenate(
            [re * turn_re - im * turn_im, re * turn_im + im * turn_re], axis=2
        )
    )


def roll_half(values):
    return pltpu.roll(values, HALF, 1)


def lane_ids(rows):
    return lax.broadcasted_iota(jnp.int32, (rows, LANES), 1)


def times_i(values):
    turned = roll_half(values)
    return jnp.where(lane_ids(values.shape[0]) < HALF, -turned, turned)


def with_i(values):
    return jnp.concatenate([values, times_i(values)], axis=0)


def dot(left, right):
    return jnp.dot(left, right, preferred_element_type=jnp.float32)


def in_vmem():
    return pl.BlockSpec(memory_space=pltpu.VMEM)


def in_hbm():
    return pl.BlockSpec(memory_space=pl.ANY)


def range_kernel(slab, fresh, filt, t1, t2, t3, t4, w_in, w_out, out, xs, os, hs, first, second, third):
    step = pl.program_id(0)

    def load(source):
        def one(n1, _):
            at = pl.ds(pl.multiple_of(n1 * LANES, LANES), LANES)
            to = pl.ds(pl.multiple_of(n1 * PITCH, 4), STEP)
            for c in range(2):
                xs[c, to, :] = source[c, :, at].astype(jnp.float32)
            return 0

        lax.fori_loop(0, RANGE_OUTER, one, 0, unroll=8)

    @pl.when(step == 0)
    def _():
        for c in range(2):
            for k2 in range(RANGE_INNER):
                hs[2 + c, k2 : k2 + 1, :] = filt[c : c + 1, k2 * LANES : (k2 + 1) * LANES]
            hs[c] = hs[2 + c].T
        load(slab)

    @pl.when(step > 0)
    def _():
        load(fresh)

    def rows(p):
        return pl.ds(p, RANGE_OUTER, stride=PITCH)

    def stage1(i, _):
        ps = (2 * i, 2 * i + 1)
        x = jnp.concatenate(
            [
                jnp.concatenate([xs[c, rows(p), :].astype(jnp.bfloat16) for p in ps], axis=1)
                for c in range(2)
            ],
            axis=0,
        )
        y = dot(t1[...], x)
        for k in range(2):
            re, im = y[:LANES, k * LANES : (k + 1) * LANES], y[LANES:, k * LANES : (k + 1) * LANES]
            at = pl.ds(pl.multiple_of((2 * i + k) * LANES, LANES), LANES)
            first[at, :LANES] = (re * w_in[0] - im * w_in[1]).astype(jnp.bfloat16)
            first[at, LANES:] = (re * w_in[1] + im * w_in[0]).astype(jnp.bfloat16)
        return 0

    def stage2(i, _):
        at = pl.ds(pl.multiple_of(2 * i * LANES, 2 * LANES), 2 * LANES)
        y = dot(first[at, :], t2[...])
        for k in range(2):
            re, im = y[k * LANES : (k + 1) * LANES, :LANES], y[k * LANES : (k + 1) * LANES, LANES:]
            at = pl.ds(pl.multiple_of((2 * i + k) * LANES, LANES), LANES)
            second[at, :LANES] = (re * hs[0] - im * hs[1]).astype(jnp.bfloat16)
            second[at, LANES:] = (re * hs[1] + im * hs[0]).astype(jnp.bfloat16)
        return 0

    def stage3(i, _):
        at = pl.ds(pl.multiple_of(2 * i * LANES, 2 * LANES), 2 * LANES)
        y = dot(second[at, :], t3[...])
        for k in range(2):
            re, im = y[k * LANES : (k + 1) * LANES, :LANES], y[k * LANES : (k + 1) * LANES, LANES:]
            cols = slice(k * LANES, (k + 1) * LANES)
            third[i, :LANES, cols] = (re * w_out[0] - im * w_out[1]).astype(jnp.bfloat16)
            third[i, LANES:, cols] = (re * w_out[1] + im * w_out[0]).astype(jnp.bfloat16)
        return 0

    def stage4(i, _):
        y = dot(t4[...], third[i])
        low = lane_ids(LANES) < HALF
        for k in range(2):
            p = 2 * i + k
            re, im = y[:LANES, k * LANES : (k + 1) * LANES], y[LANES:, k * LANES : (k + 1) * LANES]
            os[0, rows(p), :] = jnp.where(low, re, roll_half(im))
            os[1, rows(p), :] = jnp.where(low, roll_half(re), im)
        return 0

    for stage in (stage1, stage2, stage3, stage4):
        lax.fori_loop(0, STEP // 2, stage, 0, unroll=UNROLL)

    def store(n1, _):
        at = pl.ds(pl.multiple_of(n1 * PITCH, 4), STEP)
        out[n1, 0] = os[0, at, :].astype(jnp.bfloat16)
        out[n1, 1] = os[1, at, :].astype(jnp.bfloat16)
        return 0

    lax.fori_loop(0, RANGE_OUTER, store, 0, unroll=8)


def whole(shape):
    return pl.BlockSpec(shape, lambda *_: (0,) * len(shape))


def range_compress(slab, fresh, range_filter):
    tables = (
        left_table(RANGE_OUTER, -1.0),
        right_table(RANGE_INNER, -1.0),
        right_table(RANGE_INNER, 1.0),
        left_table(RANGE_OUTER, 1.0),
    )
    w_in = np.stack(twiddle(RANGE_OUTER, RANGE_INNER, RANGE_BINS, -1.0))
    w_out = np.stack(twiddle(RANGE_OUTER, RANGE_INNER, RANGE_BINS, 1.0))
    square = whole((2 * LANES, 2 * LANES))
    part = whole((2, LANES, LANES))
    out = jax.ShapeDtypeStruct((DEVICES, 2, ROWS, LANES), jnp.bfloat16)
    return pl.pallas_call(
        range_kernel,
        grid=(ROWS // STEP,),
        in_specs=[
            whole((2, STEP, RANGE_BINS)),
            pl.BlockSpec((2, STEP, RANGE_BINS), lambda i: (0, jnp.maximum(i - 1, 0), 0)),
            whole((2, RANGE_BINS)),
            square,
            square,
            square,
            square,
            part,
            part,
        ],
        out_specs=pl.BlockSpec((DEVICES, 2, STEP, LANES), lambda i: (0, 0, i, 0)),
        out_shape=out,
        scratch_shapes=[
            pltpu.VMEM((2, RANGE_OUTER * PITCH + SPARE, LANES), jnp.float32),
            pltpu.VMEM((2, RANGE_OUTER * PITCH + SPARE, LANES), jnp.float32),
            pltpu.VMEM((4, LANES, LANES), jnp.float32),
            pltpu.VMEM((STEP * LANES, 2 * LANES), jnp.bfloat16),
            pltpu.VMEM((STEP * LANES, 2 * LANES), jnp.bfloat16),
            pltpu.VMEM((STEP // 2, 2 * LANES, 2 * LANES), jnp.bfloat16),
        ],
        compiler_params=pltpu.CompilerParams(
            dimension_semantics=("arbitrary",), vmem_limit_bytes=RANGE_LIMIT * MIB
        ),
        cost_estimate=pl.CostEstimate(
            flops=4 * 2 * ROWS * RANGE_BINS * 512, bytes_accessed=8 * MIB, transcendentals=0
        ),
        name="range_compress",
    )(slab, fresh, range_filter, *tables, w_in, w_out)


def prepare_kernel(filt, taps, out, narrow, wide, fs):
    narrow[:, :BAND_MAX] = taps[...].astype(jnp.bfloat16)
    for c in range(2):
        for kl in range(PULSE_INNER):
            fs[c, kl * PITCH : kl * PITCH + STEP, :] = filt[c, kl].astype(jnp.float32)
    low = lane_ids(PULSE_INNER) < HALF
    for kb in range(STEP):
        for c in range(2):
            value = fs[c, pl.ds(kb, PULSE_INNER, stride=PITCH), :]
            turned = roll_half(value)
            at = slice(kb * PULSE_INNER, (kb + 1) * PULSE_INNER)
            out[0, c, at, :] = jnp.where(low, value, turned).astype(jnp.bfloat16)
            out[1, c, at, :] = jnp.where(low, turned, value).astype(jnp.bfloat16)

    def spread(i, _):
        at = pl.ds(pl.multiple_of(i * STEP, STEP), STEP)
        for j in range(SPREAD):
            column = jnp.broadcast_to(taps[at, j : j + 1], (STEP, LANES))
            wide[j, at, :] = column.astype(jnp.bfloat16)
        return 0

    lax.fori_loop(0, PULSE_INNER, spread, 0, unroll=4)


def prepare(azimuth_filter, taps):
    folded = azimuth_filter.reshape(2, PULSE_INNER, PULSE_OUTER, LANES)
    rows = STEP * PULSE_INNER
    return pl.pallas_call(
        prepare_kernel,
        grid=(PULSE_OUTER // STEP,),
        in_specs=[
            pl.BlockSpec((2, PULSE_INNER, STEP, LANES), lambda i: (0, 0, i, 0)),
            pl.BlockSpec((rows, BAND_MAX), lambda i: (i, 0)),
        ],
        out_specs=[
            pl.BlockSpec((2, 2, rows, LANES), lambda i: (0, 0, i, 0)),
            pl.BlockSpec((rows, LANES), lambda i: (i, 0)),
            pl.BlockSpec((SPREAD, rows, LANES), lambda i: (0, i, 0)),
        ],
        out_shape=[
            jax.ShapeDtypeStruct((2, 2, PULSES, LANES), jnp.bfloat16),
            jax.ShapeDtypeStruct((PULSES, LANES), jnp.bfloat16),
            jax.ShapeDtypeStruct((SPREAD, PULSES, LANES), jnp.bfloat16),
        ],
        scratch_shapes=[pltpu.VMEM((2, PULSE_INNER * PITCH + SPARE, LANES), jnp.float32)],
        compiler_params=pltpu.CompilerParams(
            dimension_semantics=("arbitrary",), vmem_limit_bytes=60 * MIB
        ),
        cost_estimate=pl.CostEstimate(
            flops=8 * PULSES * LANES, bytes_accessed=34 * MIB, transcendentals=0
        ),
        name="prepare",
    )(folded, taps)


def start_all(pairs, sems):
    copies = [pltpu.make_async_copy(a, b, sems.at[i]) for i, (a, b) in enumerate(pairs)]
    for copy in copies:
        copy.start()
    return copies


def then_start(copy, others):
    def run():
        copy.wait()
        for other in others:
            other.start()

    return run


def forward_steps(got, g1, t2, filt, out, ps, ts, waits):
    waits[0]()
    quarter = PULSE_INNER // STEP
    fresh_units = FRESH_ROWS // STEP

    def unpack(g, _):
        slab = pl.multiple_of(g * INNER_PITCH, 8)
        base = pl.multiple_of((FIRST_OUTER + g * fresh_units) * INNER_PITCH, 8)
        for d in range(quarter):
            block = got[g * quarter + d].astype(jnp.float32)
            ps[pl.ds(slab + d * STEP, STEP), :] = block[:STEP]
            for k in range(fresh_units):
                unit = d * fresh_units + k
                at = base + (unit // quarter) * INNER_PITCH + (unit % quarter) * STEP
                ps[pl.ds(at, STEP), :] = block[(k + 1) * STEP : (k + 2) * STEP]
        return 0

    lax.fori_loop(0, DEVICES // quarter, unpack, 0, unroll=2)

    def outer(l, _):
        x = ps[pl.ds(l, PULSE_OUTER, stride=INNER_PITCH), :]
        both = with_i(x.astype(jnp.bfloat16))
        ts[pl.ds(l, PULSE_OUTER, stride=INNER_PITCH), :] = dot(g1[l], both)
        return 0

    waits[1]()
    lax.fori_loop(0, PULSE_INNER, outer, 0, unroll=64)

    def inner(i, _):
        sides = []
        for k in range(2):
            at = pl.ds(pl.multiple_of((2 * i + k) * INNER_PITCH, 8), PULSE_INNER)
            t = ts[at, :]
            sides.append(
                with_i(t.astype(jnp.bfloat16))
            )
        y = dot(t2[...], jnp.concatenate(sides, axis=1))
        for k in range(2):
            at = pl.ds(pl.multiple_of((2 * i + k) * PULSE_INNER, PULSE_INNER), PULSE_INNER)
            cols = slice(k * LANES, (k + 1) * LANES)
            out[at, :] = (
                y[:PULSE_INNER, cols] * filt[0, at, :].astype(jnp.float32)
                + y[PULSE_INNER:, cols] * filt[1, at, :].astype(jnp.float32)
            ).astype(jnp.bfloat16)
        return 0

    waits[2]()
    return inner


def forward_kernel(
    half, got_hbm, g1_hbm, t2, filt_hbm, out_hbm, got, g1, filt, out, ps, ts, sems, out_sems
):
    copies = start_all(((got_hbm.at[:, half], got), (g1_hbm, g1)), sems)
    last = pltpu.make_async_copy(filt_hbm.at[half], filt, sems.at[2])
    waits = [then_start(copies[0], [last]), copies[1].wait, last.wait]
    inner = forward_steps(got, g1, t2, filt, out, ps, ts, waits)
    put_in_parts(inner, PULSE_OUTER // 2, 16, out, out_hbm, out_sems)


def put_in_parts(step, count, unroll, source, target, sems):
    rows = source.shape[0] // PARTS
    copies = []
    for i in range(PARTS):
        lax.fori_loop(i * count // PARTS, (i + 1) * count // PARTS, step, 0, unroll=unroll)
        at = pl.ds(i * rows, rows)
        copies.append(pltpu.make_async_copy(source.at[at], target.at[at], sems.at[i]))
        copies[i].start()
    for copy in copies:
        copy.wait()


def azimuth_forward(got, filt, half):
    g1, t2 = forward_tables()
    return pl.pallas_call(
        functools.partial(forward_kernel, half),
        in_specs=[in_hbm(), in_hbm(), in_vmem(), in_hbm()],
        out_specs=in_hbm(),
        out_shape=jax.ShapeDtypeStruct((PULSES, LANES), jnp.bfloat16),
        scratch_shapes=[
            pltpu.VMEM((DEVICES, ROWS, LANES), jnp.bfloat16),
            pltpu.VMEM(g1.shape, jnp.bfloat16),
            pltpu.VMEM((2, PULSES, LANES), jnp.bfloat16),
            pltpu.VMEM((PULSES, LANES), jnp.bfloat16),
            pltpu.VMEM((PULSE_OUTER * INNER_PITCH + SPARE, LANES), jnp.float32),
            pltpu.VMEM((PULSE_OUTER * INNER_PITCH + SPARE, LANES), jnp.float32),
            pltpu.SemaphoreType.DMA((3,)),
            pltpu.SemaphoreType.DMA((PARTS,)),
        ],
        compiler_params=pltpu.CompilerParams(vmem_limit_bytes=FWD_LIMIT * MIB),
        cost_estimate=pl.CostEstimate(
            flops=2 * PULSES * LANES * 512, bytes_accessed=12 * MIB, transcendentals=0
        ),
        name="azimuth_forward",
    )(got, g1, t2, filt)


def tap_steps():
    later = [(j, min(2, BAND_MAX - j)) for j in range(SPREAD, BAND_MAX, 2)]
    return later + [(j, 2) for j in range(0, SPREAD, 2)]


def tap_pairs(narrow_hbm, narrow, taps_hbm, taps):
    spans = [pl.ds(j, 2) for j in range(0, SPREAD, 2)]
    return [(narrow_hbm, narrow)] + [(taps_hbm.at[at], taps.at[at]) for at in spans]


def own_half(half, row):
    values = jnp.broadcast_to(row[...], (8, LANES))
    here = (lane_ids(8) < HALF) == (half == 0)
    return jnp.where(here, values, roll_half(values))[0:1]


def select_table(half, offsets, widths, sel):
    offsets, widths = own_half(half, offsets), own_half(half, widths)
    index = lax.broadcasted_iota(jnp.int32, (2 * LANES, LANES), 0)
    lane = lax.broadcasted_iota(jnp.int32, (2 * LANES, LANES), 1)
    column = jnp.where(index >= LANES, HALF, 0) + (index & (HALF - 1))
    same = ((index >> 6) & 1) == (lane >> 6)
    want = (lane & (HALF - 1)) + offsets
    for j in range(BAND_MAX):
        hit = same & (column == want + j) & (widths > j)
        sel[:, j * LANES : (j + 1) * LANES] = jnp.where(hit, 1.0, 0.0).astype(jnp.bfloat16)


def inverse_steps(
    left, right, narrow, taps, sel, g1, t2, out, out_hbm, sums, moved, vs, os, waits, out_sems
):
    size = GROUP * PULSE_INNER

    steps = tap_steps()

    def pick(order, g, _):
        j, wide = steps[order]
        at = pl.ds(pl.multiple_of(g * size, size), size)
        source = jnp.concatenate([left[at, :], right[at, :]], axis=1)
        picked = dot(source, sel[:, j * LANES : (j + wide) * LANES])
        total = None if order == 0 else sums[at, :]
        if j >= SPREAD:
            columns = narrow[at, :].astype(jnp.float32)
        for k in range(wide):
            if j >= SPREAD:
                weight = columns[:, j + k : j + k + 1]
            else:
                weight = taps[j + k, at, :].astype(jnp.float32)
            term = picked[:, k * LANES : (k + 1) * LANES] * weight
            total = term if total is None else total + term
        if order + 1 < len(steps):
            sums[at, :] = total
        else:
            moved[at, :] = total.astype(jnp.bfloat16)
        return 0

    waits[0]()
    waits[1]()
    for order, (j, _) in enumerate(steps):
        if j < SPREAD:
            waits[2 + j // 2]()
        lax.fori_loop(0, PULSE_OUTER // GROUP, functools.partial(pick, order), 0, unroll=32)

    def inner(kb, _):
        at = pl.ds(pl.multiple_of(kb * PULSE_INNER, PULSE_INNER), PULSE_INNER)
        vs[pl.ds(kb, PULSE_INNER, stride=OUTER_PITCH), :] = dot(g1[kb], with_i(moved[at, :]))
        return 0

    waits[-1]()
    lax.fori_loop(0, PULSE_OUTER, inner, 0, unroll=64)

    def last(i, _):
        sides = []
        for k in range(2):
            at = pl.ds(pl.multiple_of((2 * i + k) * OUTER_PITCH, 8), PULSE_OUTER)
            v = vs[at, :]
            sides.append(
                with_i(v.astype(jnp.bfloat16))
            )
        y = dot(t2[...], jnp.concatenate(sides, axis=1))
        for k in range(2):
            os[pl.ds(2 * i + k, KEPT_OUTER, stride=INNER_PITCH), :] = y[
                :, k * LANES : (k + 1) * LANES
            ]
        return 0

    lax.fori_loop(0, PULSE_INNER // 2, last, 0, unroll=32)

    quarter = PULSE_INNER // STEP
    fresh_units = FRESH_ROWS // STEP

    def pack(g, _):
        base = pl.multiple_of(g * fresh_units * INNER_PITCH, 8)
        for d in range(quarter):
            for k in range(fresh_units):
                unit = d * fresh_units + k
                at = (unit // quarter) * INNER_PITCH + (unit % quarter) * STEP
                out[g * quarter + d, k * STEP : (k + 1) * STEP, :] = os[
                    pl.ds(base + at, STEP), :
                ].astype(jnp.bfloat16)
        return 0

    put_in_parts(pack, DEVICES // quarter, 4, out, out_hbm, out_sems)


def inverse_kernel(
    left_hbm,
    right_hbm,
    narrow_hbm,
    taps_hbm,
    offsets,
    widths,
    g1_hbm,
    t2,
    out_hbm,
    left,
    right,
    narrow,
    taps,
    g1,
    out,
    sel,
    sums,
    moved,
    vs,
    os,
    sems,
    out_sems,
):
    pairs = [(left_hbm, left), (right_hbm, right), *tap_pairs(narrow_hbm, narrow, taps_hbm, taps), (g1_hbm, g1)]
    copies = start_all(pairs, sems)
    select_table(1, offsets, widths, sel)

    def both():
        copies[0].wait()
        copies[1].wait()

    waits = [both, *[copy.wait for copy in copies[2:]]]
    inverse_steps(
        left, right, narrow, taps, sel, g1, t2, out, out_hbm, sums, moved, vs, os, waits, out_sems
    )


def middle_kernel(
    half,
    got_hbm,
    f1_hbm,
    f2,
    filt_hbm,
    left_hbm,
    narrow_hbm,
    taps_hbm,
    offsets,
    widths,
    g1_hbm,
    t2,
    right_hbm,
    out_hbm,
    got,
    f1,
    filt,
    right,
    ps,
    ts,
    left,
    narrow,
    taps,
    g1,
    out,
    sel,
    sums,
    moved,
    sems,
    late_sems,
    right_sem,
    out_sems,
):
    first = start_all(((got_hbm.at[:, half], got), (f1_hbm, f1)), sems)
    first.append(pltpu.make_async_copy(filt_hbm.at[half], filt, sems.at[2]))
    pairs = [(left_hbm, left), *tap_pairs(narrow_hbm, narrow, taps_hbm, taps), (g1_hbm, g1)]
    late = [pltpu.make_async_copy(a, b, late_sems.at[i]) for i, (a, b) in enumerate(pairs)]
    select_table(0, offsets, widths, sel)

    cut = 4
    waits = [
        then_start(first[0], first[2:]),
        then_start(first[1], late[:cut]),
        then_start(first[2], late[cut:]),
    ]
    inner = forward_steps(got, f1, f2, filt, right, ps, ts, waits)
    lax.fori_loop(0, PULSE_OUTER // 2, inner, 0, unroll=64)
    put_right = pltpu.make_async_copy(right, right_hbm, right_sem.at[0])
    put_right.start()
    waits = [copy.wait for copy in late]
    inverse_steps(
        left, right, narrow, taps, sel, g1, t2, out, out_hbm, sums, moved, ts, ps, waits, out_sems
    )
    put_right.wait()


def forward_tables():
    re, im = dft_table(PULSE_INNER, -1.0)
    t2 = bf16(np.block([[re, im], [-im, re]]))
    return turned_tables(PULSE_OUTER, PULSE_INNER, -1.0), t2


def inverse_tables():
    re, im = dft_table(PULSE_OUTER, 1.0)
    t2 = bf16(np.concatenate([re[FIRST_OUTER:], im[FIRST_OUTER:]], axis=1))
    return turned_tables(PULSE_INNER, PULSE_OUTER, 1.0), t2


def forward_and_inverse(got, filt, half, left, narrow, taps, bands):
    f1, f2 = forward_tables()
    g1, t2 = inverse_tables()
    return pl.pallas_call(
        functools.partial(middle_kernel, half),
        in_specs=[in_hbm(), in_hbm(), in_vmem()] + [in_hbm()] * 4
        + [in_vmem(), in_vmem(), in_hbm(), in_vmem()],
        out_specs=[in_hbm(), in_hbm()],
        out_shape=[
            jax.ShapeDtypeStruct((PULSES, LANES), jnp.bfloat16),
            jax.ShapeDtypeStruct((DEVICES, FRESH_ROWS, LANES), jnp.bfloat16),
        ],
        scratch_shapes=[
            pltpu.VMEM((DEVICES, ROWS, LANES), jnp.bfloat16),
            pltpu.VMEM(f1.shape, jnp.bfloat16),
            pltpu.VMEM((2, PULSES, LANES), jnp.bfloat16),
            pltpu.VMEM((PULSES, LANES), jnp.bfloat16),
            pltpu.VMEM((PULSE_OUTER * INNER_PITCH + SPARE, LANES), jnp.float32),
            pltpu.VMEM((PULSE_OUTER * INNER_PITCH + SPARE, LANES), jnp.float32),
            pltpu.VMEM((PULSES, LANES), jnp.bfloat16),
            pltpu.VMEM((PULSES, LANES), jnp.bfloat16),
            pltpu.VMEM((SPREAD, PULSES, LANES), jnp.bfloat16),
            pltpu.VMEM(g1.shape, jnp.bfloat16),
            pltpu.VMEM((DEVICES, FRESH_ROWS, LANES), jnp.bfloat16),
            pltpu.VMEM((2 * LANES, BAND_MAX * LANES), jnp.bfloat16),
            pltpu.VMEM((PULSES, LANES), jnp.float32),
            pltpu.VMEM((PULSES, LANES), jnp.bfloat16),
            pltpu.SemaphoreType.DMA((3,)),
            pltpu.SemaphoreType.DMA((3 + SPREAD // 2,)),
            pltpu.SemaphoreType.DMA((1,)),
            pltpu.SemaphoreType.DMA((PARTS,)),
        ],
        compiler_params=pltpu.CompilerParams(vmem_limit_bytes=INV_LIMIT * MIB),
        cost_estimate=pl.CostEstimate(
            flops=2 * PULSES * LANES * (256 * BAND_MAX + 1024),
            bytes_accessed=40 * MIB,
            transcendentals=0,
        ),
        name="forward_inverse",
    )(got, f1, f2, filt, left, narrow, taps, *bands, g1, t2)


def azimuth_inverse(left, right, narrow, taps, bands):
    g1, t2 = inverse_tables()
    return pl.pallas_call(
        inverse_kernel,
        in_specs=[in_hbm()] * 4 + [in_vmem(), in_vmem(), in_hbm(), in_vmem()],
        out_specs=in_hbm(),
        out_shape=jax.ShapeDtypeStruct((DEVICES, FRESH_ROWS, LANES), jnp.bfloat16),
        scratch_shapes=[
            pltpu.VMEM((PULSES, LANES), jnp.bfloat16),
            pltpu.VMEM((PULSES, LANES), jnp.bfloat16),
            pltpu.VMEM((PULSES, LANES), jnp.bfloat16),
            pltpu.VMEM((SPREAD, PULSES, LANES), jnp.bfloat16),
            pltpu.VMEM(g1.shape, jnp.bfloat16),
            pltpu.VMEM((DEVICES, FRESH_ROWS, LANES), jnp.bfloat16),
            pltpu.VMEM((2 * LANES, BAND_MAX * LANES), jnp.bfloat16),
            pltpu.VMEM((PULSES, LANES), jnp.float32),
            pltpu.VMEM((PULSES, LANES), jnp.bfloat16),
            pltpu.VMEM((PULSE_INNER * OUTER_PITCH + SPARE, LANES), jnp.float32),
            pltpu.VMEM((KEPT_OUTER * INNER_PITCH + SPARE, LANES), jnp.float32),
            pltpu.SemaphoreType.DMA((4 + SPREAD // 2,)),
            pltpu.SemaphoreType.DMA((PARTS,)),
        ],
        compiler_params=pltpu.CompilerParams(vmem_limit_bytes=INV_LIMIT * MIB),
        cost_estimate=pl.CostEstimate(
            flops=2 * PULSES * LANES * (256 * BAND_MAX + 512),
            bytes_accessed=12 * MIB,
            transcendentals=0,
        ),
        name="migrate_inverse",
    )(left, right, narrow, taps, *bands, g1, t2)


def assemble_kernel(first_hbm, second_hbm, out_hbm, first, second, out, sems, more_sems, out_sems):
    low = lane_ids(FRESH_ROWS) < HALF
    size = RANGE_OUTER // PARTS
    spans = [pl.ds(i * size, size) for i in range(PARTS)]
    copies = start_all([(first_hbm.at[at], first.at[at]) for at in spans], sems)
    more = start_all([(second_hbm.at[at], second.at[at]) for at in spans], more_sems)

    def one(n1, _):
        a, b = first[n1].astype(jnp.float32), second[n1].astype(jnp.float32)
        at = pl.ds(pl.multiple_of(n1 * LANES, LANES), LANES)
        out[0, :, at] = jnp.where(low, a, roll_half(b)).astype(jnp.bfloat16)
        out[1, :, at] = jnp.where(low, roll_half(a), b).astype(jnp.bfloat16)
        return 0

    puts = []
    for i in range(PARTS):
        copies[i].wait()
        more[i].wait()
        lax.fori_loop(i * size, (i + 1) * size, one, 0, unroll=16)
        at = pl.ds(i * size * LANES, size * LANES)
        puts.append(pltpu.make_async_copy(out.at[:, :, at], out_hbm.at[:, :, at], out_sems.at[i]))
        puts[i].start()
    for put in puts:
        put.wait()


def assemble(first, second):
    part = pltpu.VMEM((RANGE_OUTER, FRESH_ROWS, LANES), jnp.bfloat16)
    shape = (2, FRESH_ROWS, RANGE_BINS)
    return pl.pallas_call(
        assemble_kernel,
        in_specs=[in_hbm(), in_hbm()],
        out_specs=in_hbm(),
        out_shape=jax.ShapeDtypeStruct(shape, jnp.bfloat16),
        scratch_shapes=[
            part,
            part,
            pltpu.VMEM(shape, jnp.bfloat16),
            pltpu.SemaphoreType.DMA((PARTS,)),
            pltpu.SemaphoreType.DMA((PARTS,)),
            pltpu.SemaphoreType.DMA((PARTS,)),
        ],
        compiler_params=pltpu.CompilerParams(vmem_limit_bytes=60 * MIB),
        cost_estimate=pl.CostEstimate(
            flops=4 * FRESH_ROWS * RANGE_BINS, bytes_accessed=6 * MIB, transcendentals=0
        ),
        name="assemble",
    )(first, second)


def exchanged(blocks):
    return lax.all_to_all(blocks, AXES, split_axis=0, concat_axis=0, tiled=True)


def from_next(block):
    size = lax.axis_size(AXES)
    return lax.ppermute(block, AXES, [(i + 1, i) for i in range(size - 1)])


def on_device(
    slab_echoes,
    fresh_pulses,
    range_filter,
    azimuth_filter,
    migration_taps,
    band_offsets,
    band_widths,
):
    got = exchanged(range_compress(slab_echoes, fresh_pulses, range_filter))
    taps = migration_taps.reshape(BAND_MAX, PULSE_INNER, PULSE_OUTER)
    taps = taps.transpose(2, 1, 0).reshape(PULSES, BAND_MAX)
    filt, narrow, taps = prepare(azimuth_filter, taps)
    bands = (band_offsets.reshape(1, LANES), band_widths.reshape(1, LANES))
    spectra0 = azimuth_forward(got, filt, 0)
    rim = from_next(spectra0)
    spectra1, ready0 = forward_and_inverse(got, filt, 1, spectra0, narrow, taps, bands)
    done0 = exchanged(ready0)
    done1 = exchanged(azimuth_inverse(spectra1, rim, narrow, taps, bands))
    return assemble(done0, done1)


def solution(mesh):
    placed = (
        P(None, AXES, None),
        P(None, AXES, None),
        P(),
        P(None, None, AXES),
        P(),
        P(AXES),
        P(AXES),
    )
    return jax.shard_map(
        on_device,
        mesh=mesh,
        in_specs=placed,
        out_specs=P(None, AXES, None),
        check_vma=False,
    )
```

```python
import functools
import math

import jax
import jax.numpy as jnp
import ml_dtypes
import numpy as np
from jax import lax
from jax.experimental import pallas as pl
from jax.experimental.pallas import tpu as pltpu
from jax.sharding import PartitionSpec as P

RANGE_OUTER = 128
RANGE_INNER = 128
PULSE_OUTER = 128
PULSE_INNER = 64
SLAB_PULSES = 2048
BAND_MAX = 9
RANGE_BINS = 16384
PULSES = 8192
FRESH_COUNT = 6144
LANES = 128
HALF = 64
DEVICES = 128
SLAB_ROWS = SLAB_PULSES // DEVICES
FRESH_ROWS = FRESH_COUNT // DEVICES
ROWS = SLAB_ROWS + FRESH_ROWS
STEP = 16
FIRST_OUTER = SLAB_PULSES // PULSE_INNER
KEPT_OUTER = PULSE_OUTER - FIRST_OUTER
GROUP = 4
UNROLL = 8
PITCH = STEP + 4
INNER_PITCH = PULSE_INNER + 8
OUTER_PITCH = PULSE_OUTER + 8
SPARE = 128
BLOCKS = ROWS // STEP
RANGE_LIMIT = 60
FWD_LIMIT = 60
INV_LIMIT = 60
PARTS = 4
SPREAD = 6
AXES = ("az", "rg")
MIB = 1024 * 1024


def bf16(values):
    return np.asarray(values, np.float32).astype(ml_dtypes.bfloat16)


def dft_table(length, sign):
    index = np.arange(length)
    angle = (np.outer(index, index) % length).astype(np.float32) * np.float32(
        2.0 * math.pi / length
    )
    scale = np.float32(1.0 / math.sqrt(length))
    real_part = bf16(np.cos(angle) * scale).astype(np.float32)
    imag_part = bf16(sign * np.sin(angle) * scale).astype(np.float32)
    return real_part, imag_part


def twiddle(rows_size, cols_size, total, sign):
    angle = (np.outer(np.arange(rows_size), np.arange(cols_size)) % total).astype(
        np.float32
    ) * np.float32(2.0 * math.pi / total)
    return np.cos(angle), np.float32(sign) * np.sin(angle)


def left_table(length, sign):
    re, im = dft_table(length, sign)
    return bf16(np.block([[re, -im], [im, re]]))


def right_table(length, sign):
    re, im = dft_table(length, sign)
    return bf16(np.block([[re, im], [-im, re]]))


def turned_tables(outer, inner, sign):
    re, im = dft_table(outer, sign)
    tw_re, tw_im = twiddle(outer, inner, PULSES, sign)
    turn_re, turn_im = tw_re.T[:, :, None], tw_im.T[:, :, None]
    return bf16(
        np.concatenate(
            [re * turn_re - im * turn_im, re * turn_im + im * turn_re], axis=2
        )
    )


def roll_half(values):
    return pltpu.roll(values, HALF, 1)


def lane_ids(rows):
    return lax.broadcasted_iota(jnp.int32, (rows, LANES), 1)


def times_i(values):
    turned = roll_half(values)
    return jnp.where(lane_ids(values.shape[0]) < HALF, -turned, turned)


def with_i(values):
    return jnp.concatenate([values, times_i(values)], axis=0)


def dot(left, right):
    return jnp.dot(left, right, preferred_element_type=jnp.float32)


def in_vmem():
    return pl.BlockSpec(memory_space=pltpu.VMEM)


def in_hbm():
    return pl.BlockSpec(memory_space=pl.ANY)


def range_kernel(slab, fresh, filt, t1, t2, t3, t4, w_in, w_out, out, xs, os, hs, first, second, third):
    step = pl.program_id(0)

    def load(source):
        def one(n1, _):
            at = pl.ds(pl.multiple_of(n1 * LANES, LANES), LANES)
            to = pl.ds(pl.multiple_of(n1 * PITCH, 4), STEP)
            for c in range(2):
                xs[c, to, :] = source[c, :, at].astype(jnp.float32)
            return 0

        lax.fori_loop(0, RANGE_OUTER, one, 0, unroll=32)

    @pl.when(step == 0)
    def _():
        for c in range(2):
            for k2 in range(RANGE_INNER):
                hs[2 + c, k2 : k2 + 1, :] = filt[c : c + 1, k2 * LANES : (k2 + 1) * LANES]
            hs[c] = hs[2 + c].T
        load(slab)

    @pl.when(step > 0)
    def _():
        load(fresh)

    def rows(p):
        return pl.ds(p, RANGE_OUTER, stride=PITCH)

    def stage1(i, _):
        ps = (2 * i, 2 * i + 1)
        x = jnp.concatenate(
            [
                jnp.concatenate([xs[c, rows(p), :].astype(jnp.bfloat16) for p in ps], axis=1)
                for c in range(2)
            ],
            axis=0,
        )
        y = dot(t1[...], x)
        for k in range(2):
            re, im = y[:LANES, k * LANES : (k + 1) * LANES], y[LANES:, k * LANES : (k + 1) * LANES]
            at = pl.ds(pl.multiple_of((2 * i + k) * LANES, LANES), LANES)
            first[at, :LANES] = (re * w_in[0] - im * w_in[1]).astype(jnp.bfloat16)
            first[at, LANES:] = (re * w_in[1] + im * w_in[0]).astype(jnp.bfloat16)
        return 0

    def stage2(i, _):
        at = pl.ds(pl.multiple_of(2 * i * LANES, 2 * LANES), 2 * LANES)
        y = dot(first[at, :], t2[...])
        for k in range(2):
            re, im = y[k * LANES : (k + 1) * LANES, :LANES], y[k * LANES : (k + 1) * LANES, LANES:]
            at = pl.ds(pl.multiple_of((2 * i + k) * LANES, LANES), LANES)
            second[at, :LANES] = (re * hs[0] - im * hs[1]).astype(jnp.bfloat16)
            second[at, LANES:] = (re * hs[1] + im * hs[0]).astype(jnp.bfloat16)
        return 0

    def stage3(i, _):
        at = pl.ds(pl.multiple_of(2 * i * LANES, 2 * LANES), 2 * LANES)
        y = dot(second[at, :], t3[...])
        for k in range(2):
            re, im = y[k * LANES : (k + 1) * LANES, :LANES], y[k * LANES : (k + 1) * LANES, LANES:]
            cols = slice(k * LANES, (k + 1) * LANES)
            third[i, :LANES, cols] = (re * w_out[0] - im * w_out[1]).astype(jnp.bfloat16)
            third[i, LANES:, cols] = (re * w_out[1] + im * w_out[0]).astype(jnp.bfloat16)
        return 0

    def stage4(i, _):
        y = dot(t4[...], third[i])
        low = lane_ids(LANES) < HALF
        for k in range(2):
            p = 2 * i + k
            re, im = y[:LANES, k * LANES : (k + 1) * LANES], y[LANES:, k * LANES : (k + 1) * LANES]
            os[0, rows(p), :] = jnp.where(low, re, roll_half(im))
            os[1, rows(p), :] = jnp.where(low, roll_half(re), im)
        return 0

    for stage in (stage1, stage2, stage3, stage4):
        lax.fori_loop(0, STEP // 2, stage, 0, unroll=UNROLL)

    def store(n1, _):
        at = pl.ds(pl.multiple_of(n1 * PITCH, 4), STEP)
        out[n1, 0] = os[0, at, :].astype(jnp.bfloat16)
        out[n1, 1] = os[1, at, :].astype(jnp.bfloat16)
        return 0

    lax.fori_loop(0, RANGE_OUTER, store, 0, unroll=32)


def whole(shape):
    return pl.BlockSpec(shape, lambda *_: (0,) * len(shape))


def range_compress(slab, fresh, range_filter):
    tables = (
        left_table(RANGE_OUTER, -1.0),
        right_table(RANGE_INNER, -1.0),
        right_table(RANGE_INNER, 1.0),
        left_table(RANGE_OUTER, 1.0),
    )
    w_in = np.stack(twiddle(RANGE_OUTER, RANGE_INNER, RANGE_BINS, -1.0))
    w_out = np.stack(twiddle(RANGE_OUTER, RANGE_INNER, RANGE_BINS, 1.0))
    square = whole((2 * LANES, 2 * LANES))
    part = whole((2, LANES, LANES))
    out = jax.ShapeDtypeStruct((DEVICES, 2, ROWS, LANES), jnp.bfloat16)
    return pl.pallas_call(
        range_kernel,
        grid=(ROWS // STEP,),
        in_specs=[
            whole((2, STEP, RANGE_BINS)),
            pl.BlockSpec((2, STEP, RANGE_BINS), lambda i: (0, jnp.maximum(i - 1, 0), 0)),
            whole((2, RANGE_BINS)),
            square,
            square,
            square,
            square,
            part,
            part,
        ],
        out_specs=pl.BlockSpec((DEVICES, 2, STEP, LANES), lambda i: (0, 0, i, 0)),
        out_shape=out,
        scratch_shapes=[
            pltpu.VMEM((2, RANGE_OUTER * PITCH + SPARE, LANES), jnp.float32),
            pltpu.VMEM((2, RANGE_OUTER * PITCH + SPARE, LANES), jnp.float32),
            pltpu.VMEM((4, LANES, LANES), jnp.float32),
            pltpu.VMEM((STEP * LANES, 2 * LANES), jnp.bfloat16),
            pltpu.VMEM((STEP * LANES, 2 * LANES), jnp.bfloat16),
            pltpu.VMEM((STEP // 2, 2 * LANES, 2 * LANES), jnp.bfloat16),
        ],
        compiler_params=pltpu.CompilerParams(
            dimension_semantics=("arbitrary",), vmem_limit_bytes=RANGE_LIMIT * MIB
        ),
        cost_estimate=pl.CostEstimate(
            flops=4 * 2 * ROWS * RANGE_BINS * 512, bytes_accessed=8 * MIB, transcendentals=0
        ),
        name="range_compress",
    )(slab, fresh, range_filter, *tables, w_in, w_out)


def prepare_kernel(filt, taps, out, narrow, wide, fs):
    narrow[:, :BAND_MAX] = taps[...].astype(jnp.bfloat16)
    for c in range(2):
        for kl in range(PULSE_INNER):
            fs[c, kl * PITCH : kl * PITCH + STEP, :] = filt[c, kl].astype(jnp.float32)
    low = lane_ids(PULSE_INNER) < HALF
    for kb in range(STEP):
        for c in range(2):
            value = fs[c, pl.ds(kb, PULSE_INNER, stride=PITCH), :]
            turned = roll_half(value)
            at = slice(kb * PULSE_INNER, (kb + 1) * PULSE_INNER)
            out[0, c, at, :] = jnp.where(low, value, turned).astype(jnp.bfloat16)
            out[1, c, at, :] = jnp.where(low, turned, value).astype(jnp.bfloat16)

    def spread(i, _):
        at = pl.ds(pl.multiple_of(i * STEP, STEP), STEP)
        for j in range(SPREAD):
            column = jnp.broadcast_to(taps[at, j : j + 1], (STEP, LANES))
            wide[j, at, :] = column.astype(jnp.bfloat16)
        return 0

    lax.fori_loop(0, PULSE_INNER, spread, 0, unroll=4)


def prepare(azimuth_filter, taps):
    folded = azimuth_filter.reshape(2, PULSE_INNER, PULSE_OUTER, LANES)
    rows = STEP * PULSE_INNER
    return pl.pallas_call(
        prepare_kernel,
        grid=(PULSE_OUTER // STEP,),
        in_specs=[
            pl.BlockSpec((2, PULSE_INNER, STEP, LANES), lambda i: (0, 0, i, 0)),
            pl.BlockSpec((rows, BAND_MAX), lambda i: (i, 0)),
        ],
        out_specs=[
            pl.BlockSpec((2, 2, rows, LANES), lambda i: (0, 0, i, 0)),
            pl.BlockSpec((rows, LANES), lambda i: (i, 0)),
            pl.BlockSpec((SPREAD, rows, LANES), lambda i: (0, i, 0)),
        ],
        out_shape=[
            jax.ShapeDtypeStruct((2, 2, PULSES, LANES), jnp.bfloat16),
            jax.ShapeDtypeStruct((PULSES, LANES), jnp.bfloat16),
            jax.ShapeDtypeStruct((SPREAD, PULSES, LANES), jnp.bfloat16),
        ],
        scratch_shapes=[pltpu.VMEM((2, PULSE_INNER * PITCH + SPARE, LANES), jnp.float32)],
        compiler_params=pltpu.CompilerParams(
            dimension_semantics=("arbitrary",), vmem_limit_bytes=60 * MIB
        ),
        cost_estimate=pl.CostEstimate(
            flops=8 * PULSES * LANES, bytes_accessed=34 * MIB, transcendentals=0
        ),
        name="prepare",
    )(folded, taps)


def start_all(pairs, sems):
    copies = [pltpu.make_async_copy(a, b, sems.at[i]) for i, (a, b) in enumerate(pairs)]
    for copy in copies:
        copy.start()
    return copies


def then_start(copy, others):
    def run():
        copy.wait()
        for other in others:
            other.start()

    return run


def forward_steps(got, g1, t2, filt, out, ps, ts, waits):
    waits[0]()
    quarter = PULSE_INNER // STEP
    fresh_units = FRESH_ROWS // STEP

    def unpack(g, _):
        slab = pl.multiple_of(g * INNER_PITCH, 8)
        base = pl.multiple_of((FIRST_OUTER + g * fresh_units) * INNER_PITCH, 8)
        for d in range(quarter):
            block = got[g * quarter + d].astype(jnp.float32)
            ps[pl.ds(slab + d * STEP, STEP), :] = block[:STEP]
            for k in range(fresh_units):
                unit = d * fresh_units + k
                at = base + (unit // quarter) * INNER_PITCH + (unit % quarter) * STEP
                ps[pl.ds(at, STEP), :] = block[(k + 1) * STEP : (k + 2) * STEP]
        return 0

    lax.fori_loop(0, DEVICES // quarter, unpack, 0, unroll=8)

    def outer(l, _):
        x = ps[pl.ds(l, PULSE_OUTER, stride=INNER_PITCH), :]
        both = with_i(x.astype(jnp.bfloat16))
        ts[pl.ds(l, PULSE_OUTER, stride=INNER_PITCH), :] = dot(g1[l], both)
        return 0

    waits[1]()
    lax.fori_loop(0, PULSE_INNER, outer, 0, unroll=64)

    def inner(i, _):
        sides = []
        for k in range(2):
            at = pl.ds(pl.multiple_of((2 * i + k) * INNER_PITCH, 8), PULSE_INNER)
            t = ts[at, :]
            sides.append(
                with_i(t.astype(jnp.bfloat16))
            )
        y = dot(t2[...], jnp.concatenate(sides, axis=1))
        for k in range(2):
            at = pl.ds(pl.multiple_of((2 * i + k) * PULSE_INNER, PULSE_INNER), PULSE_INNER)
            cols = slice(k * LANES, (k + 1) * LANES)
            out[at, :] = (
                y[:PULSE_INNER, cols] * filt[0, at, :].astype(jnp.float32)
                + y[PULSE_INNER:, cols] * filt[1, at, :].astype(jnp.float32)
            ).astype(jnp.bfloat16)
        return 0

    waits[2]()
    return inner


def forward_kernel(
    half, got_hbm, g1_hbm, t2, filt_hbm, out_hbm, got, g1, filt, out, ps, ts, sems, out_sems
):
    copies = start_all(((got_hbm.at[:, half], got), (g1_hbm, g1)), sems)
    last = pltpu.make_async_copy(filt_hbm.at[half], filt, sems.at[2])
    waits = [then_start(copies[0], [last]), copies[1].wait, last.wait]
    inner = forward_steps(got, g1, t2, filt, out, ps, ts, waits)
    put_in_parts(inner, PULSE_OUTER // 2, 16, out, out_hbm, out_sems)


def put_in_parts(step, count, unroll, source, target, sems):
    rows = source.shape[0] // PARTS
    copies = []
    for i in range(PARTS):
        lax.fori_loop(i * count // PARTS, (i + 1) * count // PARTS, step, 0, unroll=unroll)
        at = pl.ds(i * rows, rows)
        copies.append(pltpu.make_async_copy(source.at[at], target.at[at], sems.at[i]))
        copies[i].start()
    for copy in copies:
        copy.wait()


def azimuth_forward(got, filt, half):
    g1, t2 = forward_tables()
    return pl.pallas_call(
        functools.partial(forward_kernel, half),
        in_specs=[in_hbm(), in_hbm(), in_vmem(), in_hbm()],
        out_specs=in_hbm(),
        out_shape=jax.ShapeDtypeStruct((PULSES, LANES), jnp.bfloat16),
        scratch_shapes=[
            pltpu.VMEM((DEVICES, ROWS, LANES), jnp.bfloat16),
            pltpu.VMEM(g1.shape, jnp.bfloat16),
            pltpu.VMEM((2, PULSES, LANES), jnp.bfloat16),
            pltpu.VMEM((PULSES, LANES), jnp.bfloat16),
            pltpu.VMEM((PULSE_OUTER * INNER_PITCH + SPARE, LANES), jnp.float32),
            pltpu.VMEM((PULSE_OUTER * INNER_PITCH + SPARE, LANES), jnp.float32),
            pltpu.SemaphoreType.DMA((3,)),
            pltpu.SemaphoreType.DMA((PARTS,)),
        ],
        compiler_params=pltpu.CompilerParams(vmem_limit_bytes=FWD_LIMIT * MIB),
        cost_estimate=pl.CostEstimate(
            flops=2 * PULSES * LANES * 512, bytes_accessed=12 * MIB, transcendentals=0
        ),
        name="azimuth_forward",
    )(got, g1, t2, filt)


def tap_steps():
    later = [(j, min(2, BAND_MAX - j)) for j in range(SPREAD, BAND_MAX, 2)]
    return later + [(j, 2) for j in range(0, SPREAD, 2)]


def tap_pairs(narrow_hbm, narrow, taps_hbm, taps):
    spans = [pl.ds(j, 2) for j in range(0, SPREAD, 2)]
    return [(narrow_hbm, narrow)] + [(taps_hbm.at[at], taps.at[at]) for at in spans]


def own_half(half, row):
    values = jnp.broadcast_to(row[...], (8, LANES))
    here = (lane_ids(8) < HALF) == (half == 0)
    return jnp.where(here, values, roll_half(values))[0:1]


def select_table(half, offsets, widths, sel):
    offsets, widths = own_half(half, offsets), own_half(half, widths)
    index = lax.broadcasted_iota(jnp.int32, (2 * LANES, LANES), 0)
    lane = lax.broadcasted_iota(jnp.int32, (2 * LANES, LANES), 1)
    column = jnp.where(index >= LANES, HALF, 0) + (index & (HALF - 1))
    same = ((index >> 6) & 1) == (lane >> 6)
    want = (lane & (HALF - 1)) + offsets
    for j in range(BAND_MAX):
        hit = same & (column == want + j) & (widths > j)
        sel[:, j * LANES : (j + 1) * LANES] = jnp.where(hit, 1.0, 0.0).astype(jnp.bfloat16)


def inverse_steps(
    left, right, narrow, taps, sel, g1, t2, out, out_hbm, sums, moved, vs, os, waits, out_sems
):
    size = GROUP * PULSE_INNER

    steps = tap_steps()

    def pick(order, g, _):
        j, wide = steps[order]
        at = pl.ds(pl.multiple_of(g * size, size), size)
        source = jnp.concatenate([left[at, :], right[at, :]], axis=1)
        picked = dot(source, sel[:, j * LANES : (j + wide) * LANES])
        total = None if order == 0 else sums[at, :]
        if j >= SPREAD:
            columns = narrow[at, :].astype(jnp.float32)
        for k in range(wide):
            if j >= SPREAD:
                weight = columns[:, j + k : j + k + 1]
            else:
                weight = taps[j + k, at, :].astype(jnp.float32)
            term = picked[:, k * LANES : (k + 1) * LANES] * weight
            total = term if total is None else total + term
        if order + 1 < len(steps):
            sums[at, :] = total
        else:
            moved[at, :] = total.astype(jnp.bfloat16)
        return 0

    waits[0]()
    waits[1]()
    for order, (j, _) in enumerate(steps):
        if j < SPREAD:
            waits[2 + j // 2]()
        lax.fori_loop(0, PULSE_OUTER // GROUP, functools.partial(pick, order), 0, unroll=32)

    def inner(kb, _):
        at = pl.ds(pl.multiple_of(kb * PULSE_INNER, PULSE_INNER), PULSE_INNER)
        vs[pl.ds(kb, PULSE_INNER, stride=OUTER_PITCH), :] = dot(g1[kb], with_i(moved[at, :]))
        return 0

    waits[-1]()
    lax.fori_loop(0, PULSE_OUTER, inner, 0, unroll=64)

    def last(i, _):
        sides = []
        for k in range(2):
            at = pl.ds(pl.multiple_of((2 * i + k) * OUTER_PITCH, 8), PULSE_OUTER)
            v = vs[at, :]
            sides.append(
                with_i(v.astype(jnp.bfloat16))
            )
        y = dot(t2[...], jnp.concatenate(sides, axis=1))
        for k in range(2):
            os[pl.ds(2 * i + k, KEPT_OUTER, stride=INNER_PITCH), :] = y[
                :, k * LANES : (k + 1) * LANES
            ]
        return 0

    lax.fori_loop(0, PULSE_INNER // 2, last, 0, unroll=32)

    quarter = PULSE_INNER // STEP
    fresh_units = FRESH_ROWS // STEP

    def pack(g, _):
        base = pl.multiple_of(g * fresh_units * INNER_PITCH, 8)
        for d in range(quarter):
            for k in range(fresh_units):
                unit = d * fresh_units + k
                at = (unit // quarter) * INNER_PITCH + (unit % quarter) * STEP
                out[g * quarter + d, k * STEP : (k + 1) * STEP, :] = os[
                    pl.ds(base + at, STEP), :
                ].astype(jnp.bfloat16)
        return 0

    put_in_parts(pack, DEVICES // quarter, 4, out, out_hbm, out_sems)


def inverse_kernel(
    left_hbm,
    right_hbm,
    narrow_hbm,
    taps_hbm,
    offsets,
    widths,
    g1_hbm,
    t2,
    out_hbm,
    left,
    right,
    narrow,
    taps,
    g1,
    out,
    sel,
    sums,
    moved,
    vs,
    os,
    sems,
    out_sems,
):
    pairs = [(left_hbm, left), (right_hbm, right), *tap_pairs(narrow_hbm, narrow, taps_hbm, taps), (g1_hbm, g1)]
    copies = start_all(pairs, sems)
    select_table(1, offsets, widths, sel)

    def both():
        copies[0].wait()
        copies[1].wait()

    waits = [both, *[copy.wait for copy in copies[2:]]]
    inverse_steps(
        left, right, narrow, taps, sel, g1, t2, out, out_hbm, sums, moved, vs, os, waits, out_sems
    )


def middle_kernel(
    half,
    got_hbm,
    f1_hbm,
    f2,
    filt_hbm,
    left_hbm,
    narrow_hbm,
    taps_hbm,
    offsets,
    widths,
    g1_hbm,
    t2,
    right_hbm,
    out_hbm,
    got,
    f1,
    filt,
    right,
    ps,
    ts,
    left,
    narrow,
    taps,
    g1,
    out,
    sel,
    sums,
    moved,
    sems,
    late_sems,
    right_sem,
    out_sems,
):
    first = start_all(((got_hbm.at[:, half], got), (f1_hbm, f1)), sems)
    first.append(pltpu.make_async_copy(filt_hbm.at[half], filt, sems.at[2]))
    pairs = [(left_hbm, left), *tap_pairs(narrow_hbm, narrow, taps_hbm, taps), (g1_hbm, g1)]
    late = [pltpu.make_async_copy(a, b, late_sems.at[i]) for i, (a, b) in enumerate(pairs)]
    select_table(0, offsets, widths, sel)

    cut = 4
    waits = [
        then_start(first[0], first[2:]),
        then_start(first[1], late[:cut]),
        then_start(first[2], late[cut:]),
    ]
    inner = forward_steps(got, f1, f2, filt, right, ps, ts, waits)
    lax.fori_loop(0, PULSE_OUTER // 2, inner, 0, unroll=64)
    put_right = pltpu.make_async_copy(right, right_hbm, right_sem.at[0])
    put_right.start()
    waits = [copy.wait for copy in late]
    inverse_steps(
        left, right, narrow, taps, sel, g1, t2, out, out_hbm, sums, moved, ts, ps, waits, out_sems
    )
    put_right.wait()


def forward_tables():
    re, im = dft_table(PULSE_INNER, -1.0)
    t2 = bf16(np.block([[re, im], [-im, re]]))
    return turned_tables(PULSE_OUTER, PULSE_INNER, -1.0), t2


def inverse_tables():
    re, im = dft_table(PULSE_OUTER, 1.0)
    t2 = bf16(np.concatenate([re[FIRST_OUTER:], im[FIRST_OUTER:]], axis=1))
    return turned_tables(PULSE_INNER, PULSE_OUTER, 1.0), t2


def forward_and_inverse(got, filt, half, left, narrow, taps, bands):
    f1, f2 = forward_tables()
    g1, t2 = inverse_tables()
    return pl.pallas_call(
        functools.partial(middle_kernel, half),
        in_specs=[in_hbm(), in_hbm(), in_vmem()] + [in_hbm()] * 4
        + [in_vmem(), in_vmem(), in_hbm(), in_vmem()],
        out_specs=[in_hbm(), in_hbm()],
        out_shape=[
            jax.ShapeDtypeStruct((PULSES, LANES), jnp.bfloat16),
            jax.ShapeDtypeStruct((DEVICES, FRESH_ROWS, LANES), jnp.bfloat16),
        ],
        scratch_shapes=[
            pltpu.VMEM((DEVICES, ROWS, LANES), jnp.bfloat16),
            pltpu.VMEM(f1.shape, jnp.bfloat16),
            pltpu.VMEM((2, PULSES, LANES), jnp.bfloat16),
            pltpu.VMEM((PULSES, LANES), jnp.bfloat16),
            pltpu.VMEM((PULSE_OUTER * INNER_PITCH + SPARE, LANES), jnp.float32),
            pltpu.VMEM((PULSE_OUTER * INNER_PITCH + SPARE, LANES), jnp.float32),
            pltpu.VMEM((PULSES, LANES), jnp.bfloat16),
            pltpu.VMEM((PULSES, LANES), jnp.bfloat16),
            pltpu.VMEM((SPREAD, PULSES, LANES), jnp.bfloat16),
            pltpu.VMEM(g1.shape, jnp.bfloat16),
            pltpu.VMEM((DEVICES, FRESH_ROWS, LANES), jnp.bfloat16),
            pltpu.VMEM((2 * LANES, BAND_MAX * LANES), jnp.bfloat16),
            pltpu.VMEM((PULSES, LANES), jnp.float32),
            pltpu.VMEM((PULSES, LANES), jnp.bfloat16),
            pltpu.SemaphoreType.DMA((3,)),
            pltpu.SemaphoreType.DMA((3 + SPREAD // 2,)),
            pltpu.SemaphoreType.DMA((1,)),
            pltpu.SemaphoreType.DMA((PARTS,)),
        ],
        compiler_params=pltpu.CompilerParams(vmem_limit_bytes=INV_LIMIT * MIB),
        cost_estimate=pl.CostEstimate(
            flops=2 * PULSES * LANES * (256 * BAND_MAX + 1024),
            bytes_accessed=40 * MIB,
            transcendentals=0,
        ),
        name="forward_inverse",
    )(got, f1, f2, filt, left, narrow, taps, *bands, g1, t2)


def azimuth_inverse(left, right, narrow, taps, bands):
    g1, t2 = inverse_tables()
    return pl.pallas_call(
        inverse_kernel,
        in_specs=[in_hbm()] * 4 + [in_vmem(), in_vmem(), in_hbm(), in_vmem()],
        out_specs=in_hbm(),
        out_shape=jax.ShapeDtypeStruct((DEVICES, FRESH_ROWS, LANES), jnp.bfloat16),
        scratch_shapes=[
            pltpu.VMEM((PULSES, LANES), jnp.bfloat16),
            pltpu.VMEM((PULSES, LANES), jnp.bfloat16),
            pltpu.VMEM((PULSES, LANES), jnp.bfloat16),
            pltpu.VMEM((SPREAD, PULSES, LANES), jnp.bfloat16),
            pltpu.VMEM(g1.shape, jnp.bfloat16),
            pltpu.VMEM((DEVICES, FRESH_ROWS, LANES), jnp.bfloat16),
            pltpu.VMEM((2 * LANES, BAND_MAX * LANES), jnp.bfloat16),
            pltpu.VMEM((PULSES, LANES), jnp.float32),
            pltpu.VMEM((PULSES, LANES), jnp.bfloat16),
            pltpu.VMEM((PULSE_INNER * OUTER_PITCH + SPARE, LANES), jnp.float32),
            pltpu.VMEM((KEPT_OUTER * INNER_PITCH + SPARE, LANES), jnp.float32),
            pltpu.SemaphoreType.DMA((4 + SPREAD // 2,)),
            pltpu.SemaphoreType.DMA((PARTS,)),
        ],
        compiler_params=pltpu.CompilerParams(vmem_limit_bytes=INV_LIMIT * MIB),
        cost_estimate=pl.CostEstimate(
            flops=2 * PULSES * LANES * (256 * BAND_MAX + 512),
            bytes_accessed=12 * MIB,
            transcendentals=0,
        ),
        name="migrate_inverse",
    )(left, right, narrow, taps, *bands, g1, t2)


def assemble_kernel(first_hbm, second_hbm, out_hbm, first, second, out, sems, more_sems, out_sems):
    low = lane_ids(FRESH_ROWS) < HALF
    size = RANGE_OUTER // PARTS
    spans = [pl.ds(i * size, size) for i in range(PARTS)]
    copies = start_all([(first_hbm.at[at], first.at[at]) for at in spans], sems)
    more = start_all([(second_hbm.at[at], second.at[at]) for at in spans], more_sems)

    def one(n1, _):
        a, b = first[n1].astype(jnp.float32), second[n1].astype(jnp.float32)
        at = pl.ds(pl.multiple_of(n1 * LANES, LANES), LANES)
        out[0, :, at] = jnp.where(low, a, roll_half(b)).astype(jnp.bfloat16)
        out[1, :, at] = jnp.where(low, roll_half(a), b).astype(jnp.bfloat16)
        return 0

    puts = []
    for i in range(PARTS):
        copies[i].wait()
        more[i].wait()
        lax.fori_loop(i * size, (i + 1) * size, one, 0, unroll=32)
        at = pl.ds(i * size * LANES, size * LANES)
        puts.append(pltpu.make_async_copy(out.at[:, :, at], out_hbm.at[:, :, at], out_sems.at[i]))
        puts[i].start()
    for put in puts:
        put.wait()


def assemble(first, second):
    part = pltpu.VMEM((RANGE_OUTER, FRESH_ROWS, LANES), jnp.bfloat16)
    shape = (2, FRESH_ROWS, RANGE_BINS)
    return pl.pallas_call(
        assemble_kernel,
        in_specs=[in_hbm(), in_hbm()],
        out_specs=in_hbm(),
        out_shape=jax.ShapeDtypeStruct(shape, jnp.bfloat16),
        scratch_shapes=[
            part,
            part,
            pltpu.VMEM(shape, jnp.bfloat16),
            pltpu.SemaphoreType.DMA((PARTS,)),
            pltpu.SemaphoreType.DMA((PARTS,)),
            pltpu.SemaphoreType.DMA((PARTS,)),
        ],
        compiler_params=pltpu.CompilerParams(vmem_limit_bytes=60 * MIB),
        cost_estimate=pl.CostEstimate(
            flops=4 * FRESH_ROWS * RANGE_BINS, bytes_accessed=6 * MIB, transcendentals=0
        ),
        name="assemble",
    )(first, second)


def exchanged(blocks):
    return lax.all_to_all(blocks, AXES, split_axis=0, concat_axis=0, tiled=True)


def from_next(block):
    size = lax.axis_size(AXES)
    return lax.ppermute(block, AXES, [(i + 1, i) for i in range(size - 1)])


def on_device(
    slab_echoes,
    fresh_pulses,
    range_filter,
    azimuth_filter,
    migration_taps,
    band_offsets,
    band_widths,
):
    got = exchanged(range_compress(slab_echoes, fresh_pulses, range_filter))
    taps = migration_taps.reshape(BAND_MAX, PULSE_INNER, PULSE_OUTER)
    taps = taps.transpose(2, 1, 0).reshape(PULSES, BAND_MAX)
    filt, narrow, taps = prepare(azimuth_filter, taps)
    bands = (band_offsets.reshape(1, LANES), band_widths.reshape(1, LANES))
    spectra0 = azimuth_forward(got, filt, 0)
    rim = from_next(spectra0)
    spectra1, ready0 = forward_and_inverse(got, filt, 1, spectra0, narrow, taps, bands)
    done0 = exchanged(ready0)
    done1 = exchanged(azimuth_inverse(spectra1, rim, narrow, taps, bands))
    return assemble(done0, done1)


def solution(mesh):
    placed = (
        P(None, AXES, None),
        P(None, AXES, None),
        P(),
        P(None, None, AXES),
        P(),
        P(AXES),
        P(AXES),
    )
    return jax.shard_map(
        on_device,
        mesh=mesh,
        in_specs=placed,
        out_specs=P(None, AXES, None),
        check_vma=False,
    )
```
